32 devices in a mesh: blk: 8 (over y, x, core), tm: 4 (over z).
Axes of the slice: x: 2, y: 2, z: 4, core: 2. Of those that a mesh axis runs over, the one named last changes fastest.
Arguments:
- records: bfloat16 [2048, 16, 512], P('blk', 'tm'), may hold values from -6 to 6
- glitch_mask: int32 [2048, 16], P('blk'), may hold values 0 or 1
- fir_taps: bfloat16 [65], replicated, may hold values from -1.1953125 to 1.1953125
Outputs:
- correlations: bfloat16 [16, 2048, 2048], P('tm', 'blk')
The draws below stay inside these ranges and needn't reach their ends.
All inputs are finite; a program needn't handle non-finite values. No bound on the sum of `glitch_mask` on one device may be relied on, other than what follows from the above.
Results may differ from the reference program's by a relative error of at most 0.015.
Values may be sent and summed in bfloat16 or wider, within the bound.
A program may use at most 256 MiB of HBM per device.

```python
import math
import jax
import jax.numpy as jnp
from jax import lax

SEGLEN = 512
BINS = 128
FIRST_BIN = 16
TAPS = 65
SMOOTH = 64
LAGS = 16
BLOCK_CH = 256
CHANNELS = 2048
SEGMENTS = 16
N_BLK = 8
N_TM = 4


def touch_ends(result, rng, least, high):
    index_at = [jax.random.randint(jax.random.fold_in(rng, axis), (), 0, length) for axis, length in enumerate(result.shape)]
    widest = result.shape.index(max(result.shape))
    beside = index_at[:widest] + [(index_at[widest] + 1) % result.shape[widest]] + index_at[widest + 1:]
    return result.at[tuple(index_at)].set(least).at[tuple(beside)].set(high)


def level_of(rng, extent, shards, least, high):
    loudness, own = 1.0, jax.random.fold_in(rng, 6)
    for axis_at, shards_of in shards:
        steps = jnp.exp(jax.random.uniform(jax.random.fold_in(own, axis_at), (shards_of,), jnp.float32, least / len(shards), high / len(shards)))
        loudness = loudness * jnp.repeat(steps, extent[axis_at] // shards_of).reshape([-1 if axis == axis_at else 1 for axis in range(len(extent))])
    return loudness


def bell_draw(rng, shape, scale, bound, shards=(), kind=jnp.bfloat16):
    result = scale * jax.random.normal(rng, shape, jnp.float32)
    if shards:
        result = result * level_of(rng, shape, shards, -0.22, 0.18)
    return jnp.clip(result, -bound, bound).astype(kind)


def setup_inputs(seed: int = 0) -> dict:
    arg_keys = jax.random.split(jax.random.key(seed), 4)
    return {
        "records": bell_draw(arg_keys[0], (CHANNELS, SEGMENTS, SEGLEN), 1.0, 6.0, ((0, 8), (1, 4))),
        "glitch_mask": touch_ends((jax.random.randint(arg_keys[1], (CHANNELS, SEGMENTS), 0, 5) < 4).astype(jnp.int32), jax.random.fold_in(arg_keys[1], 1), 0, 1),
        "fir_taps": bell_draw(arg_keys[2], (TAPS,), 0.2, 1.1953125),
    }


def filter_matrix(fir_taps):
    source = lax.broadcasted_iota(jnp.int32, (SEGLEN, SEGLEN), 0)
    target = lax.broadcasted_iota(jnp.int32, (SEGLEN, SEGLEN), 1)
    offsets = source - target + (TAPS - 1) // 2
    weights = fir_taps.astype(jnp.float32)
    matrix = jnp.zeros((SEGLEN, SEGLEN), jnp.float32)
    for tap_index in range(TAPS):
        matrix = matrix + jnp.where(offsets == tap_index, weights[tap_index], jnp.float32(0.0))
    return matrix

def transform_table(fir_taps):
    sample = lax.broadcasted_iota(jnp.int32, (SEGLEN, BINS), 0)
    freq = lax.broadcasted_iota(jnp.int32, (SEGLEN, BINS), 1) + FIRST_BIN
    phase = sample * freq % SEGLEN
    angle = phase.astype(jnp.float32) * jnp.float32(2.0 * math.pi / SEGLEN)
    dft = jnp.concatenate([jnp.cos(angle), -jnp.sin(angle)], axis=1)
    combined = jnp.dot(filter_matrix(fir_taps), dft, precision=lax.Precision.HIGHEST, preferred_element_type=jnp.float32)
    return combined.astype(jnp.bfloat16)

def smoothing():
    source = lax.broadcasted_iota(jnp.int32, (SEGLEN, SEGLEN), 0)
    target = lax.broadcasted_iota(jnp.int32, (SEGLEN, SEGLEN), 1)
    inside = jnp.abs(source - target) <= SMOOTH
    band_ones = jnp.where(inside, 1.0, 0.0).astype(jnp.bfloat16)
    counts = lax.optimization_barrier(jnp.sum(jnp.where(inside, 1.0, 0.0).astype(jnp.float32), axis=0))
    return (band_ones, counts)

def whiten(samples, usable, combined, band_ones, counts):
    envelope = jnp.dot(jnp.abs(samples), band_ones, preferred_element_type=jnp.float32) / counts[None, :]
    normal = (samples.astype(jnp.float32) / (envelope + 1e-06)).astype(jnp.bfloat16)
    spectra = jnp.dot(normal, combined, preferred_element_type=jnp.float32)
    real_part = spectra[:, :BINS]
    imag_part = spectra[:, BINS:]
    power_mean = lax.optimization_barrier(jnp.mean(real_part * real_part + imag_part * imag_part, axis=1, keepdims=True))
    scale_rows = usable.astype(jnp.float32)[:, None] / jnp.sqrt(power_mean + 1e-06)
    return (spectra * scale_rows).astype(jnp.bfloat16)

def lag_tables():
    delay = lax.broadcasted_iota(jnp.int32, (LAGS, BINS), 0) - LAGS // 2
    freq = lax.broadcasted_iota(jnp.int32, (LAGS, BINS), 1) + FIRST_BIN
    phase = delay * freq % SEGLEN
    angle = phase.astype(jnp.float32) * jnp.float32(2.0 * math.pi / SEGLEN)
    factor = jnp.float32(1.0 / math.sqrt(SEGMENTS * BINS))
    return ((jnp.cos(angle) * factor).astype(jnp.bfloat16), (jnp.sin(angle) * factor).astype(jnp.bfloat16))

def reference(records, glitch_mask, fir_taps):
    combined = transform_table(fir_taps)
    band_ones, counts = smoothing()
    rows_block = BLOCK_CH * SEGMENTS
    blocks = records.reshape(N_BLK, rows_block, SEGLEN)
    masks = glitch_mask.reshape(N_BLK, rows_block)
    whitened = lax.map(lambda pair: whiten(pair[0], pair[1], combined, band_ones, counts), (blocks, masks))
    spectra = whitened.reshape(CHANNELS, SEGMENTS, 2, BINS).astype(jnp.float32)
    real_all = jnp.transpose(spectra[:, :, 0, :], (2, 1, 0))
    imag_all = jnp.transpose(spectra[:, :, 1, :], (2, 1, 0))
    cos_rows, sin_rows = lag_tables()
    band_bins = BINS // N_TM
    cos_bands = cos_rows.astype(jnp.float32).reshape(LAGS, N_TM, band_bins)
    sin_bands = sin_rows.astype(jnp.float32).reshape(LAGS, N_TM, band_bins)

    def column_block(block_index):
        start = (block_index * BLOCK_CH).astype(jnp.int32)
        other_real = lax.dynamic_slice_in_dim(real_all, start, BLOCK_CH, 2)
        other_imag = lax.dynamic_slice_in_dim(imag_all, start, BLOCK_CH, 2)
        cross_real = jnp.einsum('fsi,fsj->fij', real_all, other_real) + jnp.einsum('fsi,fsj->fij', imag_all, other_imag)
        cross_imag = jnp.einsum('fsi,fsj->fij', imag_all, other_real) - jnp.einsum('fsi,fsj->fij', real_all, other_imag)
        cross_real = lax.optimization_barrier(cross_real.astype(jnp.bfloat16)).astype(jnp.float32)
        cross_imag = lax.optimization_barrier(cross_imag.astype(jnp.bfloat16)).astype(jnp.float32)
        cross_real = cross_real.reshape(N_TM, band_bins, CHANNELS, BLOCK_CH)
        cross_imag = cross_imag.reshape(N_TM, band_bins, CHANNELS, BLOCK_CH)
        partial_terms = jnp.einsum('ltf,tfij->tlij', cos_bands, cross_real) - jnp.einsum('ltf,tfij->tlij', sin_bands, cross_imag)
        partial_terms = lax.optimization_barrier(partial_terms.astype(jnp.bfloat16)).astype(jnp.float32)
        return lax.optimization_barrier(jnp.sum(partial_terms, axis=0)).astype(jnp.bfloat16)
    columns = lax.map(column_block, jnp.arange(N_BLK, dtype=jnp.int32))
    return jnp.transpose(columns, (1, 2, 0, 3)).reshape(LAGS, CHANNELS, CHANNELS)
```

```python
import math

import jax
import jax.numpy as jnp
import numpy as np
from jax import lax
from jax.experimental import pallas as pl
from jax.experimental.pallas import tpu as pltpu
from jax.sharding import PartitionSpec as P

BINS = 128
FIRST_BIN = 16
SMOOTH = 64
LAGS = 16


def dft_thirds(seglen):
    sample = np.arange(seglen)[:, None]
    freq = np.arange(BINS)[None, :] + FIRST_BIN
    angle = (sample * freq % seglen) * (2.0 * math.pi / seglen)
    rest = np.concatenate([np.cos(angle), -np.sin(angle)], axis=1).astype(np.float32)
    thirds = []
    for _ in range(3):
        part = rest.astype(jnp.bfloat16)
        thirds.append(part)
        rest = rest - part.astype(np.float32)
    return np.concatenate(thirds, axis=1)


def lag_rows(seg_total, seglen):
    delay = np.arange(LAGS)[:, None] - LAGS // 2
    freq = np.arange(BINS)[None, :] + FIRST_BIN
    angle = (delay * freq % seglen) * (2.0 * math.pi / seglen)
    factor = 1.0 / math.sqrt(seg_total * BINS)
    tables = np.stack([np.cos(angle), np.sin(angle)]).astype(np.float32) * np.float32(factor)
    return tables.astype(jnp.bfloat16).astype(np.float32)


def filter_matrix(fir_taps, seglen):
    half = (fir_taps.shape[0] - 1) // 2
    period = 2 * seglen
    line = jnp.pad(fir_taps[::-1], (seglen - 1 - half, seglen - half))
    rows = jnp.tile(line, seglen)[: seglen * (period - 1)].reshape(seglen, period - 1)
    return rows[:, seglen - 1 :]


def transform_table(fir_taps, seglen):
    parts = jnp.dot(
        filter_matrix(fir_taps, seglen),
        jnp.asarray(dft_thirds(seglen)),
        preferred_element_type=jnp.float32,
    )
    width = 2 * BINS
    total = parts[:, :width] + (parts[:, width : 2 * width] + parts[:, 2 * width :])
    return total.astype(jnp.bfloat16)


def whiten(samples, usable, fir_taps):
    seglen = samples.shape[1]
    source = lax.broadcasted_iota(jnp.int32, (seglen, seglen), 0)
    target = lax.broadcasted_iota(jnp.int32, (seglen, seglen), 1)
    band_ones = jnp.where(jnp.abs(source - target) <= SMOOTH, 1.0, 0.0).astype(jnp.bfloat16)
    where = lax.broadcasted_iota(jnp.int32, (1, seglen), 1)
    counts = jnp.minimum(where, SMOOTH) + jnp.minimum(seglen - 1 - where, SMOOTH) + 1
    envelope = jnp.dot(
        jnp.abs(samples), band_ones, preferred_element_type=jnp.float32
    ) / counts.astype(jnp.float32)
    normal = (samples.astype(jnp.float32) / (envelope + 1e-06)).astype(jnp.bfloat16)
    spectra = jnp.dot(normal, transform_table(fir_taps, seglen), preferred_element_type=jnp.float32)
    power = jnp.sum(spectra * spectra, axis=1, keepdims=True) * jnp.float32(1.0 / BINS)
    scale = usable.astype(jnp.float32)[:, None] / jnp.sqrt(power + 1e-06)
    return (spectra * scale).astype(jnp.bfloat16)


def gathered_body(records, glitch_mask, fir_taps):
    tm_count = lax.axis_size("tm")
    tm_index = lax.axis_index("tm")
    chans, segs, seglen = records.shape
    seg_total = glitch_mask.shape[1]
    usable = lax.dynamic_slice_in_dim(glitch_mask, tm_index * segs, segs, 1)
    white = whiten(records.reshape(chans * segs, seglen), usable.reshape(chans * segs), fir_taps)
    slab = white.reshape(chans, segs * 2 * BINS)
    column = lax.all_gather(slab, "tm", axis=1, tiled=True)
    every = lax.all_gather(column, "blk", axis=0, tiled=True)
    lags_dev = LAGS // tm_count
    tables = lax.dynamic_slice_in_dim(
        jnp.asarray(lag_rows(seg_total, seglen)), tm_index * lags_dev, lags_dev, 1
    )
    cos_rows = tables[0][:, None, None, :]
    sin_rows = tables[1][:, None, None, :]
    own = column.reshape(chans, seg_total, 2, BINS).astype(jnp.float32)
    real_part, imag_part = own[None, :, :, 0], own[None, :, :, 1]
    turned = jnp.stack(
        [cos_rows * real_part - sin_rows * imag_part, cos_rows * imag_part + sin_rows * real_part],
        axis=3,
    ).astype(jnp.bfloat16)
    left = turned.reshape(lags_dev, chans, seg_total * 2 * BINS)
    return jnp.einsum("lik,jk->lij", left, every, preferred_element_type=jnp.float32).astype(
        jnp.bfloat16
    )


NEAREST = ((0, 1, 2, 3), (1, 2, 0, 3), (2, 1, 3, 0), (3, 2, 1, 0))
MESH = pl.DeviceIdType.MESH


def kernel(x_ref, use_ref, tap_ref, dft_ref, tab_ref, done, slabs, left, acc, taps, sent, got):
    chans, segs, seglen = x_ref.shape
    width = 2 * BINS
    depth = segs * width
    lags = left.shape[1]
    half = chans // 2
    part_ch = half // 2
    b, z = lax.axis_index("blk"), lax.axis_index("tm")
    core = lax.rem(b, 2)
    at_x = lax.rem(lax.div(b, 2), 2)
    at_y = lax.div(b, 4)
    sib = b + 1 - 2 * core
    by_x = b + 2 - 4 * at_x
    by_y = b + 4 - 8 * at_y
    across = by_x + 4 - 8 * at_y
    up, down = z + 1, z - 1
    has_up, has_down = z < 3, z > 0
    in_middle = jnp.logical_and(has_up, has_down)
    at_end = jnp.logical_not(in_middle)

    def guarded(when, action):
        if when is None:
            action()
        else:
            pl.when(when)(action)

    barrier = pltpu.get_barrier_semaphore()
    for block, plane, when in (
        (sib, z, None), (by_x, z, None), (by_y, z, None), (b, up, has_up), (b, down, has_down)
    ):
        guarded(
            when,
            lambda block=block, plane=plane: pl.semaphore_signal(
                barrier, inc=1, device_id=(block, plane), device_id_type=MESH
            ),
        )

    def slab_of(plane, block):
        return plane * 8 + block

    own = slab_of(z, b)
    taps[...] = jnp.zeros_like(taps)
    taps[0:1, : tap_ref.shape[1]] = tap_ref[...].astype(jnp.float32)
    middle = (tap_ref.shape[1] - 1) // 2
    period = 2 * seglen
    tap_at = lax.broadcasted_iota(jnp.int32, (128, period), 0)
    spot = lax.broadcasted_iota(jnp.int32, (128, period), 1)
    offset = middle - tap_at
    place = jnp.where(spot == jnp.where(offset < 0, offset + period, offset), 1.0, 0.0)
    line = jnp.dot(
        taps[...].astype(jnp.bfloat16), place.astype(jnp.bfloat16), preferred_element_type=jnp.float32
    )[0:1]
    line = jnp.broadcast_to(line, (seglen, period))
    fir = pltpu.roll(line, 0, 1, stride=1, stride_axis=0)[:, :seglen].astype(jnp.bfloat16)
    parts = jnp.dot(fir, dft_ref[...], preferred_element_type=jnp.float32)
    table = (parts[:, :width] + (parts[:, width : 2 * width] + parts[:, 2 * width :])).astype(jnp.bfloat16)
    source = lax.broadcasted_iota(jnp.int32, (seglen, seglen), 0)
    target = lax.broadcasted_iota(jnp.int32, (seglen, seglen), 1)
    band_ones = jnp.where(jnp.abs(source - target) <= SMOOTH, 1.0, 0.0).astype(jnp.bfloat16)
    where = lax.broadcasted_iota(jnp.int32, (1, seglen), 1)
    counts = jnp.minimum(where, SMOOTH) + jnp.minimum(seglen - 1 - where, SMOOTH) + 1
    counts = counts.astype(jnp.float32)
    rows = part_ch * segs
    to_row = lax.broadcasted_iota(jnp.int32, (rows, rows), 0)
    from_row = lax.broadcasted_iota(jnp.int32, (rows, rows), 1)
    by_segment = jnp.where(
        from_row == lax.rem(to_row, part_ch) * segs + lax.div(to_row, part_ch), 1.0, 0.0
    ).astype(jnp.bfloat16)
    wanted = lax.broadcasted_iota(jnp.int32, (use_ref.shape[0], segs * BINS), 0)
    column = lax.div(lax.broadcasted_iota(jnp.int32, (use_ref.shape[0], segs * BINS), 1), BINS)
    usable = lax.dot_general(
        use_ref[...].astype(jnp.bfloat16),
        jnp.where(wanted == z * segs + column, 1.0, 0.0).astype(jnp.bfloat16),
        (((0,), (0,)), ((), ())),
        preferred_element_type=jnp.float32,
    )

    def whiten_half(h):
        samples = x_ref[h * half : (h + 1) * half].reshape(half * segs, seglen)
        envelope = jnp.dot(jnp.abs(samples), band_ones, preferred_element_type=jnp.float32) / counts
        normal = (samples.astype(jnp.float32) / (envelope + 1e-06)).astype(jnp.bfloat16)
        spectra = jnp.dot(normal, table, preferred_element_type=jnp.float32)
        power = jnp.sum(spectra * spectra, axis=1, keepdims=True) * jnp.float32(1.0 / BINS)
        white = (spectra / jnp.sqrt(power + 1e-06)).astype(jnp.bfloat16)
        for k in range(2):
            sorted_rows = jnp.dot(
                by_segment, white[k * rows : (k + 1) * rows], preferred_element_type=jnp.float32
            )
            first = h * half + k * part_ch
            for s in range(segs):
                slabs[own, first : first + part_ch, s * width : (s + 1) * width] = (
                    sorted_rows[s * part_ch : (s + 1) * part_ch]
                    * usable[first : first + part_ch, s * BINS : s * BINS + 1]
                ).astype(jnp.bfloat16)

    sends = {}

    def make(index, slab, block, plane, h):
        ref = slabs.at[slab, pl.ds(h * half, half)]
        return pltpu.make_async_remote_copy(
            src_ref=ref, dst_ref=ref, send_sem=sent.at[index], recv_sem=got.at[slab, h],
            device_id=(block, plane), device_id_type=MESH,
        )

    def send(name, slab, block, plane, h, when=None):
        name = name + (h,)
        if name not in sends:
            sends[name] = (len(sends), slab, block, plane, h, when)
        guarded(when, lambda: make(*sends[name][:-1]).start())

    def arrive(slab, h):
        make(0, slab, sib, z, h).wait_recv()

    plane_at, onward, goes_on = [z], [None], [None]
    for step in range(1, 4):
        plane = sum(jnp.where(z == at, NEAREST[at][step], 0) for at in range(4))
        following = jnp.where(plane > z, z - 1, z + 1)
        plane_at.append(plane)
        onward.append(following)
        goes_on.append(jnp.logical_and(following >= 0, following <= 3))

    def turn(step):
        slab = slab_of(plane_at[step], b)

        def one(lag, carry):
            row = z * lags + lag
            cos_row = tab_ref[0, pl.ds(row, 1), :]
            sin_row = tab_ref[1, pl.ds(row, 1), :]
            for s in range(segs):
                at = s * width
                real_part = slabs[slab, :, at : at + BINS].astype(jnp.float32)
                imag_part = slabs[slab, :, at + BINS : at + width].astype(jnp.float32)
                left[step, lag, :, at : at + BINS] = (
                    cos_row * real_part - sin_row * imag_part
                ).astype(jnp.bfloat16)
                left[step, lag, :, at + BINS : at + width] = (
                    cos_row * imag_part + sin_row * real_part
                ).astype(jnp.bfloat16)
            return carry

        lax.fori_loop(0, lags, one, 0)

    blocks = {"b": b, "x": by_x, "y": by_y, "c": across}
    steps_done = {}

    def multiply(step, key, h):
        block = blocks[key]
        other = block + 1 - 2 * core
        arrive(slab_of(plane_at[step], other), h)
        count = steps_done.get((key, h), 0)
        steps_done[key, h] = count + 1
        pair = lax.div(block, 2) * 2
        right = slabs[pl.ds(slab_of(plane_at[step], pair), 2), h * half : (h + 1) * half]
        term = lax.dot_general(
            left[step].reshape(lags * chans, depth),
            right.reshape(2 * half, depth),
            (((1,), (1,)), ((), ())),
            preferred_element_type=jnp.float32,
        ).reshape(lags, chans, 2 * half)
        at = "bxyc".index(key) * 2 + h
        if count == 0:
            acc[at] = term
        elif count < 3:
            acc[at] += term
        else:
            total = (acc[at] + term).astype(jnp.bfloat16)
            for twin in range(2):
                first = pl.multiple_of((pair + twin) * chans + h * half, half)
                done[:, :, pl.ds(first, half)] = total[:, :, twin * half : (twin + 1) * half]

    mine, xs, ys, corners = [
        [slab_of(plane, block) for plane in plane_at] for block in (b, by_x, by_y, across)
    ]

    def z_in(step, h, when=None):
        def action():
            arrive(mine[step], h)
            send(("z", step), mine[step], b, onward[step], h, goes_on[step])
            send(("s", step), mine[step], sib, z, h)

        guarded(when, action)

    def to_x(step, h, when=None):
        guarded(when, lambda: send(("x", step), mine[step], by_x, z, h))

    def to_y(step, h, when=None):
        guarded(when, lambda: send(("y", step), mine[step], by_y, z, h))

    def xy(step, h, when=None):
        to_x(step, h, when)
        to_y(step, h, when)

    def x_in(step, h):
        arrive(xs[step], h)
        if h == 0 and step in (0, 3):
            send(("xy", step), xs[step], by_y, z, h, at_end if step else None)
        send(("xs", step), xs[step], sib, z, h)

    def y_in(step, h):
        arrive(ys[step], h)
        if h == 1 and step in (0, 3):
            send(("yx", step), ys[step], by_x, z, h, at_end if step else None)
        send(("ys", step), ys[step], sib, z, h)

    def c_in(step, h, when=None):
        def action():
            arrive(corners[step], h)
            if step == 0:
                send(("cu",), corners[step], b, up, h, has_up)
                send(("cd",), corners[step], b, down, h, has_down)
            elif step < 3:
                send(("cz", step), corners[step], b, onward[step], h, in_middle)
            send(("cs", step), corners[step], sib, z, h)

        guarded(when, action)

    for h in range(2):
        whiten_half(h)
        if h == 0:
            pl.semaphore_wait(barrier, 3 + has_up.astype(jnp.int32) + has_down.astype(jnp.int32))
        send(("u",), own, b, up, h, has_up)
        send(("d",), own, b, down, h, has_down)
        send(("x", 0), own, by_x, z, h)
        send(("y", 0), own, by_y, z, h)
        send(("s", 0), own, sib, z, h)
    turn(0)
    multiply(0, "b", 0)
    multiply(0, "b", 1)
    z_in(1, 0)
    z_in(2, 0, in_middle)
    xy(1, 0)
    x_in(0, 0)
    y_in(0, 0)
    y_in(0, 1)
    x_in(0, 1)
    z_in(1, 1)
    z_in(2, 1, in_middle)
    xy(1, 1)
    xy(2, 0, in_middle)
    xy(2, 1, in_middle)
    turn(1)
    multiply(0, "x", 0)
    multiply(0, "y", 0)
    z_in(2, 0, at_end)
    xy(2, 0, at_end)
    z_in(3, 0, in_middle)
    xy(3, 0, in_middle)
    x_in(1, 0)
    y_in(1, 0)
    multiply(0, "x", 1)
    multiply(0, "y", 1)
    multiply(1, "b", 0)
    multiply(1, "b", 1)
    z_in(2, 1, at_end)
    xy(2, 1, at_end)
    z_in(3, 1, in_middle)
    xy(3, 1, in_middle)
    c_in(0, 0)
    c_in(0, 1)
    multiply(1, "x", 0)
    multiply(1, "y", 0)
    turn(2)
    z_in(3, 0, at_end)
    c_in(1, 0, in_middle)
    c_in(2, 0, in_middle)
    x_in(1, 1)
    y_in(1, 1)
    multiply(2, "b", 0)
    multiply(2, "b", 1)
    multiply(0, "c", 0)
    multiply(0, "c", 1)
    z_in(3, 1, at_end)
    to_x(3, 0, at_end)
    to_y(3, 1, at_end)
    to_x(3, 1, at_end)
    to_y(3, 0, at_end)
    c_in(1, 1, in_middle)
    c_in(2, 1, in_middle)
    x_in(2, 0)
    y_in(2, 0)
    turn(3)
    multiply(1, "x", 1)
    multiply(1, "y", 1)
    c_in(1, 0, at_end)
    c_in(3, 0, in_middle)
    x_in(2, 1)
    y_in(2, 1)
    multiply(2, "x", 0)
    multiply(2, "y", 0)
    multiply(3, "b", 0)
    multiply(3, "b", 1)
    c_in(1, 1, at_end)
    c_in(3, 1, in_middle)
    x_in(3, 0)
    y_in(3, 1)
    multiply(2, "x", 1)
    multiply(2, "y", 1)
    multiply(1, "c", 0)
    c_in(2, 0, at_end)
    x_in(3, 1)
    y_in(3, 0)
    multiply(3, "x", 0)
    multiply(3, "y", 1)
    multiply(1, "c", 1)
    multiply(2, "c", 0)
    multiply(3, "x", 1)
    multiply(3, "y", 0)
    c_in(3, 0, at_end)
    c_in(3, 1, at_end)
    c_in(2, 1, at_end)
    multiply(3, "c", 0)
    multiply(3, "c", 1)
    multiply(2, "c", 1)

    for index, slab, block, plane, h, when in sends.values():
        guarded(when, make(index, slab, block, plane, h).wait_send)


def store(done, out_ref, sem):
    copy = pltpu.make_async_copy(done, out_ref, sem)
    copy.start()
    copy.wait()


def kernel_body(records, glitch_mask, fir_taps):
    blocks, planes = lax.axis_size("blk"), lax.axis_size("tm")
    chans, segs, seglen = records.shape
    seg_total = glitch_mask.shape[1]
    lags_dev = LAGS // planes
    depth = segs * 2 * BINS
    bf16 = jnp.bfloat16
    shape = (lags_dev, chans, chans * blocks)
    done = pl.pallas_call(
        kernel,
        out_shape=pltpu.VMEM(shape, bf16),
        in_specs=[pl.BlockSpec(memory_space=pltpu.VMEM)] * 5,
        out_specs=pl.BlockSpec(memory_space=pltpu.VMEM),
        scratch_shapes=[
            pltpu.VMEM((blocks * planes, chans, depth), bf16),
            pltpu.VMEM((planes, lags_dev, chans, depth), bf16),
            pltpu.VMEM((8, lags_dev, chans, chans), jnp.float32),
            pltpu.VMEM((8, 128), jnp.float32),
            pltpu.SemaphoreType.DMA((96,)),
            pltpu.SemaphoreType.DMA((blocks * planes, 2)),
        ],
        compiler_params=pltpu.CompilerParams(
            collective_id=0, has_side_effects=True, vmem_limit_bytes=58 * 1024 * 1024
        ),
        cost_estimate=pl.CostEstimate(
            flops=2 * lags_dev * chans * chans * blocks * planes * depth,
            bytes_accessed=2 * lags_dev * chans * chans * blocks,
            transcendentals=0,
        ),
    )(
        records,
        glitch_mask.T,
        fir_taps[None, :],
        jnp.asarray(dft_thirds(seglen)),
        jnp.asarray(lag_rows(seg_total, seglen)),
    )
    return pl.pallas_call(
        store,
        out_shape=jax.ShapeDtypeStruct(shape, bf16),
        in_specs=[pl.BlockSpec(memory_space=pltpu.VMEM)],
        out_specs=pl.BlockSpec(memory_space=pl.ANY),
        scratch_shapes=[pltpu.SemaphoreType.DMA],
        compiler_params=pltpu.CompilerParams(vmem_limit_bytes=4 * 1024 * 1024),
    )(pltpu.with_memory_space_constraint(done, pltpu.VMEM))


def solution(mesh):
    placed = (P("blk", "tm", None), P("blk", None), P())
    small = mesh.shape["blk"] == 8 and mesh.shape["tm"] == 4
    return jax.shard_map(
        kernel_body if small else gathered_body,
        mesh=mesh,
        in_specs=placed,
        out_specs=P("tm", "blk", None),
        check_vma=False,
    )
```

```python
import math

import jax
import jax.numpy as jnp
import numpy as np
from jax import lax
from jax.experimental import pallas as pl
from jax.experimental.pallas import tpu as pltpu
from jax.sharding import PartitionSpec as P

BINS = 128
FIRST_BIN = 16
SMOOTH = 64
LAGS = 16


def dft_thirds(seglen):
    sample = np.arange(seglen)[:, None]
    freq = np.arange(BINS)[None, :] + FIRST_BIN
    angle = (sample * freq % seglen) * (2.0 * math.pi / seglen)
    rest = np.concatenate([np.cos(angle), -np.sin(angle)], axis=1).astype(np.float32)
    thirds = []
    for _ in range(3):
        part = rest.astype(jnp.bfloat16)
        thirds.append(part)
        rest = rest - part.astype(np.float32)
    return np.concatenate(thirds, axis=1)


def lag_rows(seg_total, seglen):
    delay = np.arange(LAGS)[:, None] - LAGS // 2
    freq = np.arange(BINS)[None, :] + FIRST_BIN
    angle = (delay * freq % seglen) * (2.0 * math.pi / seglen)
    factor = 1.0 / math.sqrt(seg_total * BINS)
    tables = np.stack([np.cos(angle), np.sin(angle)]).astype(np.float32) * np.float32(factor)
    return tables.astype(jnp.bfloat16).astype(np.float32)


def filter_matrix(fir_taps, seglen):
    half = (fir_taps.shape[0] - 1) // 2
    period = 2 * seglen
    line = jnp.pad(fir_taps[::-1], (seglen - 1 - half, seglen - half))
    rows = jnp.tile(line, seglen)[: seglen * (period - 1)].reshape(seglen, period - 1)
    return rows[:, seglen - 1 :]


def transform_table(fir_taps, seglen):
    parts = jnp.dot(
        filter_matrix(fir_taps, seglen),
        jnp.asarray(dft_thirds(seglen)),
        preferred_element_type=jnp.float32,
    )
    width = 2 * BINS
    total = parts[:, :width] + (parts[:, width : 2 * width] + parts[:, 2 * width :])
    return total.astype(jnp.bfloat16)


def whiten(samples, usable, fir_taps):
    seglen = samples.shape[1]
    source = lax.broadcasted_iota(jnp.int32, (seglen, seglen), 0)
    target = lax.broadcasted_iota(jnp.int32, (seglen, seglen), 1)
    band_ones = jnp.where(jnp.abs(source - target) <= SMOOTH, 1.0, 0.0).astype(jnp.bfloat16)
    where = lax.broadcasted_iota(jnp.int32, (1, seglen), 1)
    counts = jnp.minimum(where, SMOOTH) + jnp.minimum(seglen - 1 - where, SMOOTH) + 1
    envelope = jnp.dot(
        jnp.abs(samples), band_ones, preferred_element_type=jnp.float32
    ) / counts.astype(jnp.float32)
    normal = (samples.astype(jnp.float32) / (envelope + 1e-06)).astype(jnp.bfloat16)
    spectra = jnp.dot(normal, transform_table(fir_taps, seglen), preferred_element_type=jnp.float32)
    power = jnp.sum(spectra * spectra, axis=1, keepdims=True) * jnp.float32(1.0 / BINS)
    scale = usable.astype(jnp.float32)[:, None] / jnp.sqrt(power + 1e-06)
    return (spectra * scale).astype(jnp.bfloat16)


def gathered_body(records, glitch_mask, fir_taps):
    tm_count = lax.axis_size("tm")
    tm_index = lax.axis_index("tm")
    chans, segs, seglen = records.shape
    seg_total = glitch_mask.shape[1]
    usable = lax.dynamic_slice_in_dim(glitch_mask, tm_index * segs, segs, 1)
    white = whiten(records.reshape(chans * segs, seglen), usable.reshape(chans * segs), fir_taps)
    slab = white.reshape(chans, segs * 2 * BINS)
    column = lax.all_gather(slab, "tm", axis=1, tiled=True)
    every = lax.all_gather(column, "blk", axis=0, tiled=True)
    lags_dev = LAGS // tm_count
    tables = lax.dynamic_slice_in_dim(
        jnp.asarray(lag_rows(seg_total, seglen)), tm_index * lags_dev, lags_dev, 1
    )
    cos_rows = tables[0][:, None, None, :]
    sin_rows = tables[1][:, None, None, :]
    own = column.reshape(chans, seg_total, 2, BINS).astype(jnp.float32)
    real_part, imag_part = own[None, :, :, 0], own[None, :, :, 1]
    turned = jnp.stack(
        [cos_rows * real_part - sin_rows * imag_part, cos_rows * imag_part + sin_rows * real_part],
        axis=3,
    ).astype(jnp.bfloat16)
    left = turned.reshape(lags_dev, chans, seg_total * 2 * BINS)
    return jnp.einsum("lik,jk->lij", left, every, preferred_element_type=jnp.float32).astype(
        jnp.bfloat16
    )


PHASES = (
    ("0b01", "0b11",),
    ("0A01", "0B01",),
    ("0A11", "0B11", "0D00", "0D10",),
    ("1b01", "1b11", "1Ds1",),
    ("1As1", "1Bs0", "2A01",),
    ("2B01", "2D00", "2D11",),
    ("2b01", "2b11", "2A11",),
    ("3Ds1",),
    ("1Dl1", "3Dl1",),
    ("2B10", "3A01", "3B00", "3A11", "3B10", "1Bl0", "1Al1", "3b01", "3b11",),
)
OWN_TURNS = (1, 0, 0, 2, 3, 0, 0, 0, 0, 4)
NEAR_TURNS = (0, 0, 1, 2, 0, 3, 0, 4, 0, 0)
JOB_CODES = [
    int(step) * 32 + "bABD".index(key) * 8 + "01sl".index(h) * 2 + int(waits)
    for line in PHASES
    for step, key, h, waits in line
]
JOB_STARTS = [sum(len(line) for line in PHASES[:at]) for at in range(len(PHASES) + 1)]
NEAREST = ((0, 1, 2, 3), (1, 2, 0, 3), (2, 1, 3, 0), (3, 2, 1, 0))
MESH = pl.DeviceIdType.MESH


def kernel(
    x_ref, use_ref, tap_ref, dft_ref, tab_ref, done,
    slabs, left, acc, tiles, taps, sent, got, sent_tile, got_tile,
):
    chans, segs, seglen = x_ref.shape
    width = 2 * BINS
    depth = segs * width
    lags = tab_ref.shape[1] // 4
    half = chans // 2
    part_ch = half // 2
    b, z = lax.axis_index("blk"), lax.axis_index("tm")
    core = lax.rem(b, 2)
    at_x = lax.rem(lax.div(b, 2), 2)
    at_y = lax.div(b, 4)
    sib = b + 1 - 2 * core
    by_x = b + 2 - 4 * at_x
    by_y = b + 4 - 8 * at_y
    across = by_x + 4 - 8 * at_y
    low = at_x == 0
    near_a, near_b = jnp.where(low, by_x, by_y), jnp.where(low, by_y, by_x)
    soon, late = at_x, 1 - at_x
    up, down = z + 1, z - 1
    partner = z + 1 - 2 * lax.rem(z, 2)
    has_up, has_down = z < 3, z > 0
    in_middle = jnp.logical_and(has_up, has_down)
    at_end = jnp.logical_not(in_middle)

    def guarded(when, action):
        if when is None:
            action()
        else:
            pl.when(when)(action)

    barrier = pltpu.get_barrier_semaphore()
    for block, plane, when in (
        (sib, z, None), (by_x, z, None), (by_y, z, None), (b, up, has_up), (b, down, has_down),
        (by_x + 1 - 2 * core, z, None), (by_y + 1 - 2 * core, z, None),
    ):
        guarded(
            when,
            lambda block=block, plane=plane: pl.semaphore_signal(
                barrier, inc=1, device_id=(block, plane), device_id_type=MESH
            ),
        )

    def slab_of(plane, block):
        return plane * 8 + block

    own = slab_of(z, b)
    taps[...] = jnp.zeros_like(taps)
    taps[0:1, : tap_ref.shape[1]] = tap_ref[...].astype(jnp.float32)
    middle = (tap_ref.shape[1] - 1) // 2
    period = 2 * seglen
    tap_at = lax.broadcasted_iota(jnp.int32, (128, period), 0)
    spot = lax.broadcasted_iota(jnp.int32, (128, period), 1)
    offset = middle - tap_at
    place = jnp.where(spot == jnp.where(offset < 0, offset + period, offset), 1.0, 0.0)
    line = jnp.dot(
        taps[...].astype(jnp.bfloat16), place.astype(jnp.bfloat16), preferred_element_type=jnp.float32
    )[0:1]
    line = jnp.broadcast_to(line, (seglen, period))
    fir = pltpu.roll(line, 0, 1, stride=1, stride_axis=0)[:, :seglen].astype(jnp.bfloat16)
    parts = jnp.dot(fir, dft_ref[...], preferred_element_type=jnp.float32)
    table = (parts[:, :width] + (parts[:, width : 2 * width] + parts[:, 2 * width :])).astype(jnp.bfloat16)
    source = lax.broadcasted_iota(jnp.int32, (seglen, seglen), 0)
    target = lax.broadcasted_iota(jnp.int32, (seglen, seglen), 1)
    band_ones = jnp.where(jnp.abs(source - target) <= SMOOTH, 1.0, 0.0).astype(jnp.bfloat16)
    where = lax.broadcasted_iota(jnp.int32, (1, seglen), 1)
    counts = jnp.minimum(where, SMOOTH) + jnp.minimum(seglen - 1 - where, SMOOTH) + 1
    counts = counts.astype(jnp.float32)
    rows = part_ch * segs
    to_row = lax.broadcasted_iota(jnp.int32, (rows, rows), 0)
    from_row = lax.broadcasted_iota(jnp.int32, (rows, rows), 1)
    by_segment = jnp.where(
        from_row == lax.rem(to_row, part_ch) * segs + lax.div(to_row, part_ch), 1.0, 0.0
    ).astype(jnp.bfloat16)
    wanted = lax.broadcasted_iota(jnp.int32, (use_ref.shape[0], segs * BINS), 0)
    column = lax.div(lax.broadcasted_iota(jnp.int32, (use_ref.shape[0], segs * BINS), 1), BINS)
    usable = lax.dot_general(
        use_ref[...].astype(jnp.bfloat16),
        jnp.where(wanted == z * segs + column, 1.0, 0.0).astype(jnp.bfloat16),
        (((0,), (0,)), ((), ())),
        preferred_element_type=jnp.float32,
    )

    def whiten_half(h):
        samples = x_ref[h * half : (h + 1) * half].reshape(half * segs, seglen)
        envelope = jnp.dot(jnp.abs(samples), band_ones, preferred_element_type=jnp.float32) / counts
        normal = (samples.astype(jnp.float32) / (envelope + 1e-06)).astype(jnp.bfloat16)
        spectra = jnp.dot(normal, table, preferred_element_type=jnp.float32)
        power = jnp.sum(spectra * spectra, axis=1, keepdims=True) * jnp.float32(1.0 / BINS)
        white = (spectra / jnp.sqrt(power + 1e-06)).astype(jnp.bfloat16)
        for k in range(2):
            sorted_rows = jnp.dot(
                by_segment, white[k * rows : (k + 1) * rows], preferred_element_type=jnp.float32
            )
            first = h * half + k * part_ch
            for s in range(segs):
                slabs[own, first : first + part_ch, s * width : (s + 1) * width] = (
                    sorted_rows[s * part_ch : (s + 1) * part_ch]
                    * usable[first : first + part_ch, s * BINS : s * BINS + 1]
                ).astype(jnp.bfloat16)

    sends = {}

    def half_of(h):
        return {"s": soon, "l": late}[h] if isinstance(h, str) else h

    def part(h):
        return pl.ds(h * half if isinstance(h, int) else pl.multiple_of(h * half, half), half)

    def make(index, slab, block, plane, h):
        ref = slabs.at[slab, part(half_of(h))]
        return pltpu.make_async_remote_copy(
            src_ref=ref, dst_ref=ref, send_sem=sent.at[index], recv_sem=got.at[slab, half_of(h)],
            device_id=(block, plane), device_id_type=MESH,
        )

    def send(name, slab, block, plane, h, when=None):
        if (name, h) not in sends:
            sends[name, h] = (len(sends), slab, block, plane, h, when)
        guarded(when, lambda: make(*sends[name, h][:-1]).start())

    def arrive(slab, h, when=None):
        guarded(when, lambda: make(0, slab, sib, z, h).wait_recv())

    plane_at, onward = [z], [None]
    for step in range(1, 4):
        plane = sum(jnp.where(z == at, NEAREST[at][step], 0) for at in range(4))
        plane_at.append(plane)
        onward.append(jnp.where(plane > z, z - 1, z + 1))

    def pick(values, index):
        return sum(jnp.where(index == at, value, 0) for at, value in enumerate(values))

    def turn(step):
        slab = slab_of(pick(plane_at, step), b)

        def one(lag, carry):
            row = z * lags + lag
            cos_row = tab_ref[0, pl.ds(row, 1), :]
            sin_row = tab_ref[1, pl.ds(row, 1), :]
            for s in range(segs):
                at = s * width
                real_part = slabs[slab, :, at : at + BINS].astype(jnp.float32)
                imag_part = slabs[slab, :, at + BINS : at + width].astype(jnp.float32)
                left[step, lag, :, at : at + BINS] = (
                    cos_row * real_part - sin_row * imag_part
                ).astype(jnp.bfloat16)
                left[step, lag, :, at + BINS : at + width] = (
                    cos_row * imag_part + sin_row * real_part
                ).astype(jnp.bfloat16)
            return carry

        lax.fori_loop(0, lags, one, 0)

    def turn_both(step):
        slab = slab_of(pick(plane_at, step), near_a)

        def one(lag, carry):
            row = z * lags + lag
            cos_row = tab_ref[0, pl.ds(row, 1), :]
            sin_row = tab_ref[1, pl.ds(row, 1), :]
            group, place = lax.div(lag, 2), part(lax.rem(lag, 2))
            for s in range(segs):
                at = s * width
                real_part = slabs[slab, part(soon), at : at + BINS].astype(jnp.float32)
                imag_part = slabs[slab, part(soon), at + BINS : at + width].astype(jnp.float32)
                cos_real, sin_imag = cos_row * real_part, sin_row * imag_part
                cos_imag, sin_real = cos_row * imag_part, sin_row * real_part
                for way, (first, second) in enumerate(
                    ((cos_real - sin_imag, cos_imag + sin_real), (cos_real + sin_imag, cos_imag - sin_real))
                ):
                    to = left.at[4 + step, way * lags // 2 + group, place]
                    to[:, at : at + BINS] = first.astype(jnp.bfloat16)
                    to[:, at + BINS : at + width] = second.astype(jnp.bfloat16)
            return carry

        lax.fori_loop(0, lags, one, 0)

    def pair_of(block):
        return lax.div(block, 2) * 2

    def job(at, carry):
        code = pick(JOB_CODES, at)
        step, key = lax.div(code, 32), lax.rem(lax.div(code, 8), 4)
        h = pick((0, 1, soon, late), lax.rem(lax.div(code, 2), 4))
        plane = pick(plane_at, step)
        block = pick((b, near_a, near_b, near_b), key)
        arrive(slab_of(plane, block + 1 - 2 * core), h, lax.rem(code, 2) == 1)
        right = slabs[pl.ds(slab_of(plane, pair_of(block)), 2), part(h)]
        term = lax.dot_general(
            left[step + jnp.where(key == 3, 4, 0)].reshape(lags * chans, depth),
            right.reshape(2 * half, depth),
            (((1,), (1,)), ((), ())),
            preferred_element_type=jnp.float32,
        )
        acc[key * 2 + h] += term.reshape(lags, chans, 2 * half)
        return carry

    def finish(at, carry):
        key, h = lax.div(at, 2), lax.rem(at, 2)
        pair = pair_of(pick((b, near_a, near_b), key))
        total = acc[at].astype(jnp.bfloat16)
        for other in range(2):
            first = pl.multiple_of((pair + other) * chans + h * half, half)
            done[:, :, pl.ds(first, half)] = total[:, :, other * half : (other + 1) * half]
        return carry

    def clear(at, carry):
        acc[at] = jnp.zeros(acc.shape[1:], jnp.float32)
        return carry

    pair_b, pair_across = pair_of(near_b), pair_of(across)

    def spot_of(row_half, block, column_half):
        column = pl.multiple_of(block * chans + column_half * half, half)
        return done.at[:, pl.ds(pl.multiple_of(row_half * half, half), half), pl.ds(column, half)]

    def tile_copy(kind, h, t):
        if kind == 0:
            block, spot, at = near_a, spot_of(soon, pair_b + t, h), soon * 4 + h * 2 + t
        else:
            block, spot, at = pair_b + t, spot_of(h, near_a, soon), soon * 4 + h * 2 + core
        return pltpu.make_async_remote_copy(
            src_ref=tiles.at[kind, h, t], dst_ref=spot, send_sem=sent_tile.at[kind * 4 + h * 2 + t],
            recv_sem=got_tile.at[at], device_id=(block, z), device_id_type=MESH,
        )

    def emit(h):
        total = acc[6 + h].reshape(2, lags, half, 2 * half)
        for t in range(2):
            tiles[0, h, t] = total[0, :, :, t * half : (t + 1) * half].astype(jnp.bfloat16)
        for t in range(2):
            tile_copy(0, h, t).start()
        for t in range(2):
            for lag in range(lags):
                tiles[1, h, t, lag] = total[1, lag, :, t * half : (t + 1) * half].T.astype(jnp.bfloat16)
        for t in range(2):
            tile_copy(1, h, t).start()

    mine, slabs_a, slabs_b = [
        [slab_of(plane, block) for plane in plane_at] for block in (b, near_a, near_b)
    ]

    def z_in(step, h, when=None):
        arrive(mine[step], h, when)
        if when is not at_end:
            send(("on", step), mine[step], b, onward[step], h, in_middle)
        send(("z", step, when is at_end), mine[step], sib, z, h, when)

    def xy(step, h, when):
        send(("x", step, when is at_end), mine[step], by_x, z, h, when)
        send(("y", step, when is at_end), mine[step], by_y, z, h, when)

    def take(key, step, h):
        slab = (slabs_a if key == "A" else slabs_b)[step]
        arrive(slab, h)
        if step == 0:
            send((key, "p"), slab, b, partner, h, at_end)
        send((key, step), slab, sib, z, h)

    def land_1():
        z_in(1, 0)
        z_in(2, 0, in_middle)
        xy(1, 0, in_middle)
        take("A", 0, 0)
        take("B", 0, 0)

    def land_2():
        z_in(1, 1)
        z_in(2, 1, in_middle)
        send(("x", 1, True), mine[1], by_x, z, "l", at_end)
        send(("y", 1, True), mine[1], by_y, z, "s", at_end)
        xy(1, 1, in_middle)
        take("A", 0, 1)
        take("B", 0, 1)

    def land_3():
        z_in(2, 0, at_end)
        xy(2, 0, at_end)
        z_in(3, 0, in_middle)
        xy(3, 0, in_middle)
        take("A", 1, "s")
        take("B", 1, "s")

    def land_4():
        z_in(2, 1, at_end)
        xy(2, 1, at_end)
        z_in(3, 1, in_middle)
        xy(3, 1, in_middle)
        send(("B", "m"), slabs_b[0], b, partner, "l", in_middle)
        send(("A", "m"), slabs_a[0], b, partner, "l", in_middle)
        take("A", 2, 0)
        take("B", 2, 0)

    def land_5():
        z_in(3, 0, at_end)
        xy(3, 0, at_end)
        take("A", 2, 1)
        take("B", 2, 1)

    def land_6():
        z_in(3, 1, at_end)
        xy(3, 1, at_end)
        take("A", 3, 0)
        take("B", 3, 0)

    def land_7():
        take("A", 3, 1)
        take("B", 3, 1)
        take("B", 1, "l")

    def land_9():
        take("A", 1, "l")

    landings = {1: land_1, 2: land_2, 3: land_3, 4: land_4, 5: land_5, 6: land_6, 7: land_7, 9: land_9}

    def phase(k, carry):
        for at, land in landings.items():
            pl.when(k == at)(land)
        own_step, near_step = pick(OWN_TURNS, k), pick(NEAR_TURNS, k)
        pl.when(own_step > 0)(lambda: turn(own_step - 1))
        pl.when(near_step > 0)(lambda: turn_both(near_step - 1))
        lax.fori_loop(pick(JOB_STARTS, k), pick(JOB_STARTS[1:], k), job, 0)
        pl.when(jnp.logical_and(k >= 7, k <= 8))(lambda: emit(jnp.where(k == 7, soon, late)))
        return carry

    for h in range(2):
        whiten_half(h)
        if h == 0:
            pl.semaphore_wait(barrier, 5 + has_up.astype(jnp.int32) + has_down.astype(jnp.int32))
        send(("up",), own, b, up, h, has_up)
        send(("down",), own, b, down, h, has_down)
        send(("x", 0), own, by_x, z, h)
        send(("y", 0), own, by_y, z, h)
        send(("s", 0), own, sib, z, h)
    lax.fori_loop(0, acc.shape[0], clear, 0)
    lax.fori_loop(0, len(OWN_TURNS), phase, 0)
    lax.fori_loop(0, 6, finish, 0)

    for side in range(2):
        for h in range(2):
            for t in range(2):
                spot = spot_of(
                    jnp.where(low, h, side), pair_across + t, jnp.where(low, side, h)
                )
                pltpu.make_async_remote_copy(
                    src_ref=tiles.at[0, 0, 0], dst_ref=spot, send_sem=sent_tile.at[0],
                    recv_sem=got_tile.at[side * 4 + h * 2 + t], device_id=(sib, z), device_id_type=MESH,
                ).wait_recv()
    for index, slab, block, plane, h, when in sends.values():
        guarded(when, make(index, slab, block, plane, h).wait_send)
    for kind in range(2):
        for h in range(2):
            for t in range(2):
                tile_copy(kind, h, t).wait_send()


def store(done, out_ref, sem):
    copy = pltpu.make_async_copy(done, out_ref, sem)
    copy.start()
    copy.wait()


def kernel_body(records, glitch_mask, fir_taps):
    blocks, planes = lax.axis_size("blk"), lax.axis_size("tm")
    chans, segs, seglen = records.shape
    seg_total = glitch_mask.shape[1]
    lags_dev = LAGS // planes
    depth = segs * 2 * BINS
    half = chans // 2
    bf16 = jnp.bfloat16
    shape = (lags_dev, chans, chans * blocks)
    done = pl.pallas_call(
        kernel,
        out_shape=pltpu.VMEM(shape, bf16),
        in_specs=[pl.BlockSpec(memory_space=pltpu.VMEM)] * 5,
        out_specs=pl.BlockSpec(memory_space=pltpu.VMEM),
        scratch_shapes=[
            pltpu.VMEM((blocks * planes, chans, depth), bf16),
            pltpu.VMEM((2 * planes, lags_dev, chans, depth), bf16),
            pltpu.VMEM((8, lags_dev, chans, chans), jnp.float32),
            pltpu.VMEM((2, 2, 2, lags_dev, half, half), bf16),
            pltpu.VMEM((8, 128), jnp.float32),
            pltpu.SemaphoreType.DMA((96,)),
            pltpu.SemaphoreType.DMA((blocks * planes, 2)),
            pltpu.SemaphoreType.DMA((8,)),
            pltpu.SemaphoreType.DMA((8,)),
        ],
        compiler_params=pltpu.CompilerParams(
            collective_id=0, has_side_effects=True, vmem_limit_bytes=58 * 1024 * 1024
        ),
        cost_estimate=pl.CostEstimate(
            flops=2 * lags_dev * chans * chans * blocks * planes * depth,
            bytes_accessed=2 * lags_dev * chans * chans * blocks,
            transcendentals=0,
        ),
    )(
        records,
        glitch_mask.T,
        fir_taps[None, :],
        jnp.asarray(dft_thirds(seglen)),
        jnp.asarray(lag_rows(seg_total, seglen)),
    )
    return pl.pallas_call(
        store,
        out_shape=jax.ShapeDtypeStruct(shape, bf16),
        in_specs=[pl.BlockSpec(memory_space=pltpu.VMEM)],
        out_specs=pl.BlockSpec(memory_space=pl.ANY),
        scratch_shapes=[pltpu.SemaphoreType.DMA],
        compiler_params=pltpu.CompilerParams(vmem_limit_bytes=4 * 1024 * 1024),
    )(pltpu.with_memory_space_constraint(done, pltpu.VMEM))


def solution(mesh):
    placed = (P("blk", "tm", None), P("blk", None), P())
    small = mesh.shape["blk"] == 8 and mesh.shape["tm"] == 4
    return jax.shard_map(
        kernel_body if small else gathered_body,
        mesh=mesh,
        in_specs=placed,
        out_specs=P("tm", "blk", None),
        check_vma=False,
    )
```

```python
import math

import jax
import jax.numpy as jnp
import numpy as np
from jax import lax
from jax.experimental import pallas as pl
from jax.experimental.pallas import tpu as pltpu
from jax.sharding import PartitionSpec as P

BINS = 128
FIRST_BIN = 16
SMOOTH = 64
LAGS = 16


def dft_thirds(seglen):
    sample = np.arange(seglen)[:, None]
    freq = np.arange(BINS)[None, :] + FIRST_BIN
    angle = (sample * freq % seglen) * (2.0 * math.pi / seglen)
    rest = np.concatenate([np.cos(angle), -np.sin(angle)], axis=1).astype(np.float32)
    thirds = []
    for _ in range(3):
        part = rest.astype(jnp.bfloat16)
        thirds.append(part)
        rest = rest - part.astype(np.float32)
    return np.concatenate(thirds, axis=1)


def lag_rows(seg_total, seglen):
    delay = np.arange(LAGS)[:, None] - LAGS // 2
    freq = np.arange(BINS)[None, :] + FIRST_BIN
    angle = (delay * freq % seglen) * (2.0 * math.pi / seglen)
    factor = 1.0 / math.sqrt(seg_total * BINS)
    tables = np.stack([np.cos(angle), np.sin(angle)]).astype(np.float32) * np.float32(factor)
    return tables.astype(jnp.bfloat16).astype(np.float32)


def filter_matrix(fir_taps, seglen):
    half = (fir_taps.shape[0] - 1) // 2
    period = 2 * seglen
    line = jnp.pad(fir_taps[::-1], (seglen - 1 - half, seglen - half))
    rows = jnp.tile(line, seglen)[: seglen * (period - 1)].reshape(seglen, period - 1)
    return rows[:, seglen - 1 :]


def transform_table(fir_taps, seglen):
    parts = jnp.dot(
        filter_matrix(fir_taps, seglen),
        jnp.asarray(dft_thirds(seglen)),
        preferred_element_type=jnp.float32,
    )
    width = 2 * BINS
    total = parts[:, :width] + (parts[:, width : 2 * width] + parts[:, 2 * width :])
    return total.astype(jnp.bfloat16)


def whiten(samples, usable, fir_taps):
    seglen = samples.shape[1]
    source = lax.broadcasted_iota(jnp.int32, (seglen, seglen), 0)
    target = lax.broadcasted_iota(jnp.int32, (seglen, seglen), 1)
    band_ones = jnp.where(jnp.abs(source - target) <= SMOOTH, 1.0, 0.0).astype(jnp.bfloat16)
    where = lax.broadcasted_iota(jnp.int32, (1, seglen), 1)
    counts = jnp.minimum(where, SMOOTH) + jnp.minimum(seglen - 1 - where, SMOOTH) + 1
    envelope = jnp.dot(
        jnp.abs(samples), band_ones, preferred_element_type=jnp.float32
    ) / counts.astype(jnp.float32)
    normal = (samples.astype(jnp.float32) / (envelope + 1e-06)).astype(jnp.bfloat16)
    spectra = jnp.dot(normal, transform_table(fir_taps, seglen), preferred_element_type=jnp.float32)
    power = jnp.sum(spectra * spectra, axis=1, keepdims=True) * jnp.float32(1.0 / BINS)
    scale = usable.astype(jnp.float32)[:, None] / jnp.sqrt(power + 1e-06)
    return (spectra * scale).astype(jnp.bfloat16)


def gathered_body(records, glitch_mask, fir_taps):
    tm_count = lax.axis_size("tm")
    tm_index = lax.axis_index("tm")
    chans, segs, seglen = records.shape
    seg_total = glitch_mask.shape[1]
    usable = lax.dynamic_slice_in_dim(glitch_mask, tm_index * segs, segs, 1)
    white = whiten(records.reshape(chans * segs, seglen), usable.reshape(chans * segs), fir_taps)
    slab = white.reshape(chans, segs * 2 * BINS)
    column = lax.all_gather(slab, "tm", axis=1, tiled=True)
    every = lax.all_gather(column, "blk", axis=0, tiled=True)
    lags_dev = LAGS // tm_count
    tables = lax.dynamic_slice_in_dim(
        jnp.asarray(lag_rows(seg_total, seglen)), tm_index * lags_dev, lags_dev, 1
    )
    cos_rows = tables[0][:, None, None, :]
    sin_rows = tables[1][:, None, None, :]
    own = column.reshape(chans, seg_total, 2, BINS).astype(jnp.float32)
    real_part, imag_part = own[None, :, :, 0], own[None, :, :, 1]
    turned = jnp.stack(
        [cos_rows * real_part - sin_rows * imag_part, cos_rows * imag_part + sin_rows * real_part],
        axis=3,
    ).astype(jnp.bfloat16)
    left = turned.reshape(lags_dev, chans, seg_total * 2 * BINS)
    return jnp.einsum("lik,jk->lij", left, every, preferred_element_type=jnp.float32).astype(
        jnp.bfloat16
    )


END_PHASES = (
    ("0b01", "0b11",),
    ("0A01", "0B01",),
    ("0A11", "0B11", "0D00", "0D10",),
    ("1b01", "1b11", "1D01",),
    ("1As1", "1B00", "2A01",),
    ("2B01", "2D00", "2D11",),
    ("2b01", "2b11", "2A11", "2B10",),
    ("3D01",),
    ("1D11", "3D11",),
    ("3A01", "3B00", "3A11", "3B10", "1B10", "1Al1", "3b01", "3b11",),
)
MIDDLE_PHASES = (
    ("0b01", "0b11",),
    ("0A01", "0B01",),
    ("0A11", "0B11", "0D00", "0D10",),
    ("1b01", "1b11", "1D01",),
    ("1As1", "1B00", "2A01",),
    ("2B01", "2D00", "2b01", "2b11",),
    ("2D11",),
    ("3D01",),
    ("1D11", "3D11",),
    ("2A11", "2B10", "3A01", "3B00", "3A11", "3B10", "1B10", "1Al1", "3b01", "3b11",),
)
END_TURNS = (1, 0, 0, 2, 3, 0, 4, 0, 0, 0)
MIDDLE_TURNS = (1, 0, 0, 2, 3, 0, 0, 0, 0, 4)
NEAR_TURNS = (0, 0, 1, 2, 0, 3, 0, 4, 0, 0)


def job_codes(phases):
    return [
        int(step) * 32 + "bABD".index(key) * 8 + "01sl".index(h) * 2 + int(waits)
        for line in phases
        for step, key, h, waits in line
    ]


def job_starts(phases):
    return [sum(len(line) for line in phases[:at]) for at in range(len(phases) + 1)]


NEAREST = ((0, 1, 2, 3), (1, 2, 0, 3), (2, 1, 3, 0), (3, 2, 1, 0))
MESH = pl.DeviceIdType.MESH


def kernel(
    x_ref, use_ref, tap_ref, dft_ref, tab_ref, done,
    slabs, left, acc, tiles, taps, sent, got, sent_tile, got_tile,
):
    chans, segs, seglen = x_ref.shape
    width = 2 * BINS
    depth = segs * width
    lags = tab_ref.shape[1] // 4
    half = chans // 2
    part_ch = half // 2
    b, z = lax.axis_index("blk"), lax.axis_index("tm")
    core = lax.rem(b, 2)
    at_x = lax.rem(lax.div(b, 2), 2)
    at_y = lax.div(b, 4)
    sib = b + 1 - 2 * core
    by_x = b + 2 - 4 * at_x
    by_y = b + 4 - 8 * at_y
    across = by_x + 4 - 8 * at_y
    low, high = at_x == 0, at_x == 1
    near_a, near_b = jnp.where(low, by_x, by_y), jnp.where(low, by_y, by_x)
    soon, late = at_x, 1 - at_x
    up, down = z + 1, z - 1
    partner = z + 1 - 2 * lax.rem(z, 2)
    has_up, has_down = z < 3, z > 0
    in_middle = jnp.logical_and(has_up, has_down)
    at_end = jnp.logical_not(in_middle)

    def guarded(when, action):
        if when is None:
            action()
        else:
            pl.when(when)(action)

    barrier = pltpu.get_barrier_semaphore()
    for block, plane, when in (
        (sib, z, None), (by_x, z, None), (by_y, z, None), (b, up, has_up), (b, down, has_down),
        (by_x + 1 - 2 * core, z, None), (by_y + 1 - 2 * core, z, None),
    ):
        guarded(
            when,
            lambda block=block, plane=plane: pl.semaphore_signal(
                barrier, inc=1, device_id=(block, plane), device_id_type=MESH
            ),
        )

    def slab_of(plane, block):
        return plane * 8 + block

    own = slab_of(z, b)
    taps[...] = jnp.zeros_like(taps)
    taps[0:1, : tap_ref.shape[1]] = tap_ref[...].astype(jnp.float32)
    middle = (tap_ref.shape[1] - 1) // 2
    period = 2 * seglen
    tap_at = lax.broadcasted_iota(jnp.int32, (128, period), 0)
    spot = lax.broadcasted_iota(jnp.int32, (128, period), 1)
    offset = middle - tap_at
    place = jnp.where(spot == jnp.where(offset < 0, offset + period, offset), 1.0, 0.0)
    line = jnp.dot(
        taps[...].astype(jnp.bfloat16), place.astype(jnp.bfloat16), preferred_element_type=jnp.float32
    )[0:1]
    line = jnp.broadcast_to(line, (seglen, period))
    fir = pltpu.roll(line, 0, 1, stride=1, stride_axis=0)[:, :seglen].astype(jnp.bfloat16)
    parts = jnp.dot(fir, dft_ref[...], preferred_element_type=jnp.float32)
    table = (parts[:, :width] + (parts[:, width : 2 * width] + parts[:, 2 * width :])).astype(jnp.bfloat16)
    source = lax.broadcasted_iota(jnp.int32, (seglen, seglen), 0)
    target = lax.broadcasted_iota(jnp.int32, (seglen, seglen), 1)
    band_ones = jnp.where(jnp.abs(source - target) <= SMOOTH, 1.0, 0.0).astype(jnp.bfloat16)
    where = lax.broadcasted_iota(jnp.int32, (1, seglen), 1)
    counts = jnp.minimum(where, SMOOTH) + jnp.minimum(seglen - 1 - where, SMOOTH) + 1
    counts = counts.astype(jnp.float32)
    rows = part_ch * segs
    to_row = lax.broadcasted_iota(jnp.int32, (rows, rows), 0)
    from_row = lax.broadcasted_iota(jnp.int32, (rows, rows), 1)
    by_segment = jnp.where(
        from_row == lax.rem(to_row, part_ch) * segs + lax.div(to_row, part_ch), 1.0, 0.0
    ).astype(jnp.bfloat16)
    wanted = lax.broadcasted_iota(jnp.int32, (use_ref.shape[0], segs * BINS), 0)
    column = lax.div(lax.broadcasted_iota(jnp.int32, (use_ref.shape[0], segs * BINS), 1), BINS)
    usable = lax.dot_general(
        use_ref[...].astype(jnp.bfloat16),
        jnp.where(wanted == z * segs + column, 1.0, 0.0).astype(jnp.bfloat16),
        (((0,), (0,)), ((), ())),
        preferred_element_type=jnp.float32,
    )

    def whiten_half(h):
        samples = x_ref[h * half : (h + 1) * half].reshape(half * segs, seglen)
        envelope = jnp.dot(jnp.abs(samples), band_ones, preferred_element_type=jnp.float32) / counts
        normal = (samples.astype(jnp.float32) / (envelope + 1e-06)).astype(jnp.bfloat16)
        spectra = jnp.dot(normal, table, preferred_element_type=jnp.float32)
        power = jnp.sum(spectra * spectra, axis=1, keepdims=True) * jnp.float32(1.0 / BINS)
        white = (spectra / jnp.sqrt(power + 1e-06)).astype(jnp.bfloat16)
        for k in range(2):
            sorted_rows = jnp.dot(
                by_segment, white[k * rows : (k + 1) * rows], preferred_element_type=jnp.float32
            )
            first = h * half + k * part_ch
            for s in range(segs):
                slabs[own, first : first + part_ch, s * width : (s + 1) * width] = (
                    sorted_rows[s * part_ch : (s + 1) * part_ch]
                    * usable[first : first + part_ch, s * BINS : s * BINS + 1]
                ).astype(jnp.bfloat16)

    sends = {}

    def half_of(h):
        return {"s": soon, "l": late}[h] if isinstance(h, str) else h

    def part(h):
        return pl.ds(h * half if isinstance(h, int) else pl.multiple_of(h * half, half), half)

    def make(index, slab, block, plane, h):
        ref = slabs.at[slab, part(half_of(h))]
        return pltpu.make_async_remote_copy(
            src_ref=ref, dst_ref=ref, send_sem=sent.at[index], recv_sem=got.at[slab, half_of(h)],
            device_id=(block, plane), device_id_type=MESH,
        )

    def send(name, slab, block, plane, h, when=None):
        if (name, h) not in sends:
            sends[name, h] = (len(sends), slab, block, plane, h, when)
        guarded(when, lambda: make(*sends[name, h][:-1]).start())

    def arrive(slab, h, when=None):
        guarded(when, lambda: make(0, slab, sib, z, h).wait_recv())

    plane_at, onward = [z], [None]
    for step in range(1, 4):
        plane = sum(jnp.where(z == at, NEAREST[at][step], 0) for at in range(4))
        plane_at.append(plane)
        onward.append(jnp.where(plane > z, z - 1, z + 1))

    def pick(values, index):
        return sum(jnp.where(index == at, value, 0) for at, value in enumerate(values))

    def turn(step):
        slab = slab_of(pick(plane_at, step), b)

        def one(lag, carry):
            row = z * lags + lag
            cos_row = tab_ref[0, pl.ds(row, 1), :]
            sin_row = tab_ref[1, pl.ds(row, 1), :]
            for s in range(segs):
                at = s * width
                real_part = slabs[slab, :, at : at + BINS].astype(jnp.float32)
                imag_part = slabs[slab, :, at + BINS : at + width].astype(jnp.float32)
                left[step, lag, :, at : at + BINS] = (
                    cos_row * real_part - sin_row * imag_part
                ).astype(jnp.bfloat16)
                left[step, lag, :, at + BINS : at + width] = (
                    cos_row * imag_part + sin_row * real_part
                ).astype(jnp.bfloat16)
            return carry

        lax.fori_loop(0, lags, one, 0)

    def turn_both(step):
        slab = slab_of(pick(plane_at, step), near_a)

        def one(lag, carry):
            row = z * lags + lag
            cos_row = tab_ref[0, pl.ds(row, 1), :]
            sin_row = tab_ref[1, pl.ds(row, 1), :]
            group, place = lax.div(lag, 2), part(lax.rem(lag, 2))
            for s in range(segs):
                at = s * width
                real_part = slabs[slab, part(soon), at : at + BINS].astype(jnp.float32)
                imag_part = slabs[slab, part(soon), at + BINS : at + width].astype(jnp.float32)
                cos_real, sin_imag = cos_row * real_part, sin_row * imag_part
                cos_imag, sin_real = cos_row * imag_part, sin_row * real_part
                for way, (first, second) in enumerate(
                    ((cos_real - sin_imag, cos_imag + sin_real), (cos_real + sin_imag, cos_imag - sin_real))
                ):
                    to = left.at[4 + step, way * lags // 2 + group, place]
                    to[:, at : at + BINS] = first.astype(jnp.bfloat16)
                    to[:, at + BINS : at + width] = second.astype(jnp.bfloat16)
            return carry

        lax.fori_loop(0, lags, one, 0)

    def pair_of(block):
        return lax.div(block, 2) * 2

    def by_place(end, middle):
        return [
            one if one == two else jnp.where(in_middle, two, one) for one, two in zip(end, middle)
        ]

    codes = by_place(job_codes(END_PHASES), job_codes(MIDDLE_PHASES))
    starts = by_place(job_starts(END_PHASES), job_starts(MIDDLE_PHASES))
    own_turns = by_place(END_TURNS, MIDDLE_TURNS)

    def job(at, carry):
        code = pick(codes, at)
        step, key = lax.div(code, 32), lax.rem(lax.div(code, 8), 4)
        h = pick((0, 1, soon, late), lax.rem(lax.div(code, 2), 4))
        plane = pick(plane_at, step)
        block = pick((b, near_a, near_b, near_b), key)
        arrive(slab_of(plane, block + 1 - 2 * core), h, lax.rem(code, 2) == 1)
        right = slabs[pl.ds(slab_of(plane, pair_of(block)), 2), part(h)]
        term = lax.dot_general(
            left[step + jnp.where(key == 3, 4, 0)].reshape(lags * chans, depth),
            right.reshape(2 * half, depth),
            (((1,), (1,)), ((), ())),
            preferred_element_type=jnp.float32,
        )
        acc[key * 2 + h] += term.reshape(lags, chans, 2 * half)
        return carry

    def finish(at, carry):
        key, h = lax.div(at, 2), lax.rem(at, 2)
        pair = pair_of(pick((b, near_a, near_b), key))
        total = acc[at].astype(jnp.bfloat16)
        for other in range(2):
            first = pl.multiple_of((pair + other) * chans + h * half, half)
            done[:, :, pl.ds(first, half)] = total[:, :, other * half : (other + 1) * half]
        return carry

    def clear(at, carry):
        acc[at] = jnp.zeros(acc.shape[1:], jnp.float32)
        return carry

    pair_b, pair_across = pair_of(near_b), pair_of(across)

    def spot_of(row_half, block, column_half):
        column = pl.multiple_of(block * chans + column_half * half, half)
        return done.at[:, pl.ds(pl.multiple_of(row_half * half, half), half), pl.ds(column, half)]

    def tile_copy(kind, h, t):
        if kind == 0:
            block, spot, at = near_a, spot_of(soon, pair_b + t, h), soon * 4 + h * 2 + t
        else:
            block, spot, at = pair_b + t, spot_of(h, near_a, soon), soon * 4 + h * 2 + core
        return pltpu.make_async_remote_copy(
            src_ref=tiles.at[kind, h, t], dst_ref=spot, send_sem=sent_tile.at[kind * 4 + h * 2 + t],
            recv_sem=got_tile.at[at], device_id=(block, z), device_id_type=MESH,
        )

    def emit(h):
        total = acc[6 + h].reshape(2, lags, half, 2 * half)
        for t in range(2):
            tiles[0, h, t] = total[0, :, :, t * half : (t + 1) * half].astype(jnp.bfloat16)
        for t in range(2):
            tile_copy(0, h, t).start()
        for t in range(2):
            for lag in range(lags):
                tiles[1, h, t, lag] = total[1, lag, :, t * half : (t + 1) * half].T.astype(jnp.bfloat16)
            tile_copy(1, h, t).start()

    mine, slabs_a, slabs_b = [
        [slab_of(plane, block) for plane in plane_at] for block in (b, near_a, near_b)
    ]

    def z_in(step, h, when=None):
        arrive(mine[step], h, when)
        if when is not at_end:
            send(("on", step), mine[step], b, onward[step], h, in_middle)
        send(("z", step, when is at_end), mine[step], sib, z, h, when)

    def xy(step, h, when):
        send(("x", step, when is at_end), mine[step], by_x, z, h, when)
        send(("y", step, when is at_end), mine[step], by_y, z, h, when)

    def take(key, step, h, when=None):
        slab = (slabs_a if key == "A" else slabs_b)[step]
        arrive(slab, h, when)
        if step == 0:
            send((key, "p"), slab, b, partner, h, at_end)
        send((key, step, when is at_end, when is low), slab, sib, z, h, when)

    def land_1():
        z_in(1, 0)
        z_in(2, 0, in_middle)
        xy(1, 0, in_middle)
        take("A", 0, 0)
        take("B", 0, 0)

    def land_2():
        z_in(1, 1)
        z_in(2, 1, in_middle)
        send(("x", 1, True), mine[1], by_x, z, 0, at_end)
        send(("y", 1, True), mine[1], by_y, z, "s", at_end)
        xy(1, 1, in_middle)
        take("A", 0, 1)
        take("B", 0, 1)

    def land_3():
        z_in(2, 0, at_end)
        xy(2, 0, at_end)
        z_in(3, 0, in_middle)
        xy(3, 0, in_middle)
        take("A", 1, "s")
        take("B", 1, 0)

    def land_4():
        z_in(2, 1, at_end)
        xy(2, 1, at_end)
        z_in(3, 1, in_middle)
        xy(3, 1, in_middle)
        send(("B", "m"), slabs_b[0], b, partner, 1, in_middle)
        send(("A", "m"), slabs_a[0], b, partner, "l", in_middle)
        take("A", 2, 0)
        take("B", 2, 0)

    def land_5():
        z_in(3, 0, at_end)
        xy(3, 0, at_end)
        take("A", 2, 1)
        take("B", 2, 1, at_end)

    def land_6():
        z_in(3, 1, at_end)
        xy(3, 1, at_end)
        take("A", 3, 0)
        take("B", 3, 0)
        take("B", 2, 1, in_middle)

    def land_7():
        take("A", 3, 1, high)

    def land_8():
        take("A", 3, 1, low)
        take("B", 3, 1)
        take("B", 1, 1)

    def land_9():
        take("A", 1, "l")

    landings = {1: land_1, 2: land_2, 3: land_3, 4: land_4, 5: land_5, 6: land_6, 7: land_7, 8: land_8, 9: land_9}

    def phase(k, carry):
        for at, land in landings.items():
            pl.when(k == at)(land)
        own_step, near_step = pick(own_turns, k), pick(NEAR_TURNS, k)
        pl.when(own_step > 0)(lambda: turn(own_step - 1))
        pl.when(near_step > 0)(lambda: turn_both(near_step - 1))
        lax.fori_loop(pick(starts, k), pick(starts[1:], k), job, 0)
        pl.when(jnp.logical_and(k >= 7, k <= 8))(lambda: emit(k - 7))
        return carry

    for h in range(2):
        whiten_half(h)
        if h == 0:
            pl.semaphore_wait(barrier, 5 + has_up.astype(jnp.int32) + has_down.astype(jnp.int32))
        send(("up",), own, b, up, h, has_up)
        send(("down",), own, b, down, h, has_down)
        send(("x", 0), own, by_x, z, h)
        send(("y", 0), own, by_y, z, h)
        send(("s", 0), own, sib, z, h)
    lax.fori_loop(0, acc.shape[0], clear, 0)
    lax.fori_loop(0, len(END_TURNS), phase, 0)
    lax.fori_loop(0, 6, finish, 0)

    for side in range(2):
        for h in range(2):
            for t in range(2):
                spot = spot_of(
                    jnp.where(low, h, side), pair_across + t, jnp.where(low, side, h)
                )
                pltpu.make_async_remote_copy(
                    src_ref=tiles.at[0, 0, 0], dst_ref=spot, send_sem=sent_tile.at[0],
                    recv_sem=got_tile.at[side * 4 + h * 2 + t], device_id=(sib, z), device_id_type=MESH,
                ).wait_recv()
    for index, slab, block, plane, h, when in sends.values():
        guarded(when, make(index, slab, block, plane, h).wait_send)
    for kind in range(2):
        for h in range(2):
            for t in range(2):
                tile_copy(kind, h, t).wait_send()


def store(done, out_ref, sem):
    copies = [
        pltpu.make_async_copy(done.at[lag], out_ref.at[lag], sem.at[lag]) for lag in range(done.shape[0])
    ]
    for copy in copies:
        copy.start()
    for copy in copies:
        copy.wait()


def kernel_body(records, glitch_mask, fir_taps):
    blocks, planes = lax.axis_size("blk"), lax.axis_size("tm")
    chans, segs, seglen = records.shape
    seg_total = glitch_mask.shape[1]
    lags_dev = LAGS // planes
    depth = segs * 2 * BINS
    half = chans // 2
    bf16 = jnp.bfloat16
    shape = (lags_dev, chans, chans * blocks)
    done = pl.pallas_call(
        kernel,
        out_shape=pltpu.VMEM(shape, bf16),
        in_specs=[pl.BlockSpec(memory_space=pltpu.VMEM)] * 5,
        out_specs=pl.BlockSpec(memory_space=pltpu.VMEM),
        scratch_shapes=[
            pltpu.VMEM((blocks * planes, chans, depth), bf16),
            pltpu.VMEM((2 * planes, lags_dev, chans, depth), bf16),
            pltpu.VMEM((8, lags_dev, chans, chans), jnp.float32),
            pltpu.VMEM((2, 2, 2, lags_dev, half, half), bf16),
            pltpu.VMEM((8, 128), jnp.float32),
            pltpu.SemaphoreType.DMA((96,)),
            pltpu.SemaphoreType.DMA((blocks * planes, 2)),
            pltpu.SemaphoreType.DMA((8,)),
            pltpu.SemaphoreType.DMA((8,)),
        ],
        compiler_params=pltpu.CompilerParams(
            collective_id=0, has_side_effects=True, vmem_limit_bytes=58 * 1024 * 1024
        ),
        cost_estimate=pl.CostEstimate(
            flops=2 * lags_dev * chans * chans * blocks * planes * depth,
            bytes_accessed=2 * lags_dev * chans * chans * blocks,
            transcendentals=0,
        ),
    )(
        records,
        glitch_mask.T,
        fir_taps[None, :],
        jnp.asarray(dft_thirds(seglen)),
        jnp.asarray(lag_rows(seg_total, seglen)),
    )
    return pl.pallas_call(
        store,
        out_shape=jax.ShapeDtypeStruct(shape, bf16),
        in_specs=[pl.BlockSpec(memory_space=pltpu.VMEM)],
        out_specs=pl.BlockSpec(memory_space=pl.ANY),
        scratch_shapes=[pltpu.SemaphoreType.DMA((lags_dev,))],
        compiler_params=pltpu.CompilerParams(vmem_limit_bytes=4 * 1024 * 1024),
    )(pltpu.with_memory_space_constraint(done, pltpu.VMEM))


def solution(mesh):
    placed = (P("blk", "tm", None), P("blk", None), P())
    small = mesh.shape["blk"] == 8 and mesh.shape["tm"] == 4
    return jax.shard_map(
        kernel_body if small else gathered_body,
        mesh=mesh,
        in_specs=placed,
        out_specs=P("tm", "blk", None),
        check_vma=False,
    )
```

```python
import math

import jax
import jax.numpy as jnp
import numpy as np
from jax import lax
from jax.experimental import pallas as pl
from jax.experimental.pallas import tpu as pltpu
from jax.sharding import PartitionSpec as P

BINS = 128
FIRST_BIN = 16
SMOOTH = 64
LAGS = 16


def dft_thirds(seglen):
    sample = np.arange(seglen)[:, None]
    freq = np.arange(BINS)[None, :] + FIRST_BIN
    angle = (sample * freq % seglen) * (2.0 * math.pi / seglen)
    rest = np.concatenate([np.cos(angle), -np.sin(angle)], axis=1).astype(np.float32)
    thirds = []
    for _ in range(3):
        part = rest.astype(jnp.bfloat16)
        thirds.append(part)
        rest = rest - part.astype(np.float32)
    return np.concatenate(thirds, axis=1)


def lag_rows(seg_total, seglen):
    delay = np.arange(LAGS)[:, None] - LAGS // 2
    freq = np.arange(BINS)[None, :] + FIRST_BIN
    angle = (delay * freq % seglen) * (2.0 * math.pi / seglen)
    factor = 1.0 / math.sqrt(seg_total * BINS)
    tables = np.stack([np.cos(angle), np.sin(angle)]).astype(np.float32) * np.float32(factor)
    return tables.astype(jnp.bfloat16).astype(np.float32)


def filter_matrix(fir_taps, seglen):
    half = (fir_taps.shape[0] - 1) // 2
    period = 2 * seglen
    line = jnp.pad(fir_taps[::-1], (seglen - 1 - half, seglen - half))
    rows = jnp.tile(line, seglen)[: seglen * (period - 1)].reshape(seglen, period - 1)
    return rows[:, seglen - 1 :]


def transform_table(fir_taps, seglen):
    parts = jnp.dot(
        filter_matrix(fir_taps, seglen),
        jnp.asarray(dft_thirds(seglen)),
        preferred_element_type=jnp.float32,
    )
    width = 2 * BINS
    total = parts[:, :width] + (parts[:, width : 2 * width] + parts[:, 2 * width :])
    return total.astype(jnp.bfloat16)


def whiten(samples, usable, fir_taps):
    seglen = samples.shape[1]
    source = lax.broadcasted_iota(jnp.int32, (seglen, seglen), 0)
    target = lax.broadcasted_iota(jnp.int32, (seglen, seglen), 1)
    band_ones = jnp.where(jnp.abs(source - target) <= SMOOTH, 1.0, 0.0).astype(jnp.bfloat16)
    where = lax.broadcasted_iota(jnp.int32, (1, seglen), 1)
    counts = jnp.minimum(where, SMOOTH) + jnp.minimum(seglen - 1 - where, SMOOTH) + 1
    envelope = jnp.dot(
        jnp.abs(samples), band_ones, preferred_element_type=jnp.float32
    ) / counts.astype(jnp.float32)
    normal = (samples.astype(jnp.float32) / (envelope + 1e-06)).astype(jnp.bfloat16)
    spectra = jnp.dot(normal, transform_table(fir_taps, seglen), preferred_element_type=jnp.float32)
    power = jnp.sum(spectra * spectra, axis=1, keepdims=True) * jnp.float32(1.0 / BINS)
    scale = usable.astype(jnp.float32)[:, None] / jnp.sqrt(power + 1e-06)
    return (spectra * scale).astype(jnp.bfloat16)


def gathered_body(records, glitch_mask, fir_taps):
    tm_count = lax.axis_size("tm")
    tm_index = lax.axis_index("tm")
    chans, segs, seglen = records.shape
    seg_total = glitch_mask.shape[1]
    usable = lax.dynamic_slice_in_dim(glitch_mask, tm_index * segs, segs, 1)
    white = whiten(records.reshape(chans * segs, seglen), usable.reshape(chans * segs), fir_taps)
    slab = white.reshape(chans, segs * 2 * BINS)
    column = lax.all_gather(slab, "tm", axis=1, tiled=True)
    every = lax.all_gather(column, "blk", axis=0, tiled=True)
    lags_dev = LAGS // tm_count
    tables = lax.dynamic_slice_in_dim(
        jnp.asarray(lag_rows(seg_total, seglen)), tm_index * lags_dev, lags_dev, 1
    )
    cos_rows = tables[0][:, None, None, :]
    sin_rows = tables[1][:, None, None, :]
    own = column.reshape(chans, seg_total, 2, BINS).astype(jnp.float32)
    real_part, imag_part = own[None, :, :, 0], own[None, :, :, 1]
    turned = jnp.stack(
        [cos_rows * real_part - sin_rows * imag_part, cos_rows * imag_part + sin_rows * real_part],
        axis=3,
    ).astype(jnp.bfloat16)
    left = turned.reshape(lags_dev, chans, seg_total * 2 * BINS)
    return jnp.einsum("lik,jk->lij", left, every, preferred_element_type=jnp.float32).astype(
        jnp.bfloat16
    )


END_PHASES = (
    ("0b01", "0b11",),
    ("0A01", "0B01",),
    ("0A11", "0B11", "0D00", "0D10",),
    ("1b01", "1b11", "1D01",),
    ("1As1", "1B00", "2A01",),
    ("2B01", "2D00", "2D11", "2b01",),
    ("2b11", "2A11", "2B10",),
    ("3D01",),
    ("3A01", "3D11", "1D11",),
    ("3B00", "3A11", "3B10", "1B10", "1Al1", "3b01", "3b11",),
)
MIDDLE_PHASES = (
    ("0b01", "0b11",),
    ("0A01", "0B01",),
    ("0A11", "0B11", "0D00", "0D10",),
    ("1b01", "1b11", "1D01",),
    ("1As1", "1B00", "2A01",),
    ("2B01", "2D00", "2b01", "2b11",),
    ("2D11",),
    ("3D01",),
    ("3A01", "3D11", "1D11",),
    ("2A11", "2B10", "3B00", "3A11", "3B10", "1B10", "1Al1", "3b01", "3b11",),
)
END_TURNS = (1, 0, 0, 2, 3, 0, 4, 0, 0, 0)
MIDDLE_TURNS = (1, 0, 0, 2, 3, 0, 0, 0, 4, 0)
NEAR_TURNS = (0, 0, 1, 2, 0, 3, 0, 4, 0, 0)


def job_codes(phases):
    return [
        int(step) * 32 + "bABD".index(key) * 8 + "01sl".index(h) * 2 + int(waits)
        for line in phases
        for step, key, h, waits in line
    ]


def job_starts(phases):
    return [sum(len(line) for line in phases[:at]) for at in range(len(phases) + 1)]


NEAREST = ((0, 1, 2, 3), (1, 2, 0, 3), (2, 1, 3, 0), (3, 2, 1, 0))
MESH = pl.DeviceIdType.MESH


def kernel(
    x_ref, use_ref, tap_ref, dft_ref, tab_ref, done,
    slabs, left, acc, tiles, taps, sent, got, sent_tile, got_tile,
):
    chans, segs, seglen = x_ref.shape
    width = 2 * BINS
    depth = segs * width
    lags = tab_ref.shape[1] // 4
    half = chans // 2
    part_ch = half // 2
    b, z = lax.axis_index("blk"), lax.axis_index("tm")
    core = lax.rem(b, 2)
    at_x = lax.rem(lax.div(b, 2), 2)
    at_y = lax.div(b, 4)
    sib = b + 1 - 2 * core
    by_x = b + 2 - 4 * at_x
    by_y = b + 4 - 8 * at_y
    across = by_x + 4 - 8 * at_y
    low, high = at_x == 0, at_x == 1
    near_a, near_b = jnp.where(low, by_x, by_y), jnp.where(low, by_y, by_x)
    soon, late = at_x, 1 - at_x
    up, down = z + 1, z - 1
    partner = z + 1 - 2 * lax.rem(z, 2)
    has_up, has_down = z < 3, z > 0
    in_middle = jnp.logical_and(has_up, has_down)
    at_end = jnp.logical_not(in_middle)

    def guarded(when, action):
        if when is None:
            action()
        else:
            pl.when(when)(action)

    barrier = pltpu.get_barrier_semaphore()
    for block, plane, when in (
        (sib, z, None), (by_x, z, None), (by_y, z, None), (b, up, has_up), (b, down, has_down),
        (by_x + 1 - 2 * core, z, None), (by_y + 1 - 2 * core, z, None),
    ):
        guarded(
            when,
            lambda block=block, plane=plane: pl.semaphore_signal(
                barrier, inc=1, device_id=(block, plane), device_id_type=MESH
            ),
        )

    def slab_of(plane, block):
        return plane * 8 + block

    own = slab_of(z, b)
    taps[...] = jnp.zeros_like(taps)
    taps[0:1, : tap_ref.shape[1]] = tap_ref[...].astype(jnp.float32)
    middle = (tap_ref.shape[1] - 1) // 2
    period = 2 * seglen
    tap_at = lax.broadcasted_iota(jnp.int32, (128, period), 0)
    spot = lax.broadcasted_iota(jnp.int32, (128, period), 1)
    offset = middle - tap_at
    place = jnp.where(spot == jnp.where(offset < 0, offset + period, offset), 1.0, 0.0)
    line = jnp.dot(
        taps[...].astype(jnp.bfloat16), place.astype(jnp.bfloat16), preferred_element_type=jnp.float32
    )[0:1]
    line = jnp.broadcast_to(line, (seglen, period))
    fir = pltpu.roll(line, 0, 1, stride=1, stride_axis=0)[:, :seglen].astype(jnp.bfloat16)
    parts = jnp.dot(fir, dft_ref[...], preferred_element_type=jnp.float32)
    table = (parts[:, :width] + (parts[:, width : 2 * width] + parts[:, 2 * width :])).astype(jnp.bfloat16)
    source = lax.broadcasted_iota(jnp.int32, (seglen, seglen), 0)
    target = lax.broadcasted_iota(jnp.int32, (seglen, seglen), 1)
    band_ones = jnp.where(jnp.abs(source - target) <= SMOOTH, 1.0, 0.0).astype(jnp.bfloat16)
    where = lax.broadcasted_iota(jnp.int32, (1, seglen), 1)
    counts = jnp.minimum(where, SMOOTH) + jnp.minimum(seglen - 1 - where, SMOOTH) + 1
    counts = counts.astype(jnp.float32)
    rows = part_ch * segs
    to_row = lax.broadcasted_iota(jnp.int32, (rows, rows), 0)
    from_row = lax.broadcasted_iota(jnp.int32, (rows, rows), 1)
    by_segment = jnp.where(
        from_row == lax.rem(to_row, part_ch) * segs + lax.div(to_row, part_ch), 1.0, 0.0
    ).astype(jnp.bfloat16)
    wanted = lax.broadcasted_iota(jnp.int32, (use_ref.shape[0], segs * BINS), 0)
    column = lax.div(lax.broadcasted_iota(jnp.int32, (use_ref.shape[0], segs * BINS), 1), BINS)
    usable = lax.dot_general(
        use_ref[...].astype(jnp.bfloat16),
        jnp.where(wanted == z * segs + column, 1.0, 0.0).astype(jnp.bfloat16),
        (((0,), (0,)), ((), ())),
        preferred_element_type=jnp.float32,
    )

    def whiten_half(h):
        samples = x_ref[h * half : (h + 1) * half].reshape(half * segs, seglen)
        envelope = jnp.dot(jnp.abs(samples), band_ones, preferred_element_type=jnp.float32) / counts
        normal = (samples.astype(jnp.float32) / (envelope + 1e-06)).astype(jnp.bfloat16)
        spectra = jnp.dot(normal, table, preferred_element_type=jnp.float32)
        power = jnp.sum(spectra * spectra, axis=1, keepdims=True) * jnp.float32(1.0 / BINS)
        white = (spectra / jnp.sqrt(power + 1e-06)).astype(jnp.bfloat16)
        for k in range(2):
            sorted_rows = jnp.dot(
                by_segment, white[k * rows : (k + 1) * rows], preferred_element_type=jnp.float32
            )
            first = h * half + k * part_ch
            for s in range(segs):
                slabs[own, first : first + part_ch, s * width : (s + 1) * width] = (
                    sorted_rows[s * part_ch : (s + 1) * part_ch]
                    * usable[first : first + part_ch, s * BINS : s * BINS + 1]
                ).astype(jnp.bfloat16)

    sends = {}

    def half_of(h):
        return {"s": soon, "l": late}[h] if isinstance(h, str) else h

    def part(h):
        return pl.ds(h * half if isinstance(h, int) else pl.multiple_of(h * half, half), half)

    def make(index, slab, block, plane, h):
        ref = slabs.at[slab, part(half_of(h))]
        return pltpu.make_async_remote_copy(
            src_ref=ref, dst_ref=ref, send_sem=sent.at[index], recv_sem=got.at[slab, half_of(h)],
            device_id=(block, plane), device_id_type=MESH,
        )

    def send(name, slab, block, plane, h, when=None):
        if (name, h) not in sends:
            sends[name, h] = (len(sends), slab, block, plane, h, when)
        guarded(when, lambda: make(*sends[name, h][:-1]).start())

    def arrive(slab, h, when=None):
        guarded(when, lambda: make(0, slab, sib, z, h).wait_recv())

    plane_at, onward = [z], [None]
    for step in range(1, 4):
        plane = sum(jnp.where(z == at, NEAREST[at][step], 0) for at in range(4))
        plane_at.append(plane)
        onward.append(jnp.where(plane > z, z - 1, z + 1))

    def pick(values, index):
        return sum(jnp.where(index == at, value, 0) for at, value in enumerate(values))

    def rows_of(at):
        lag, s = lax.div(at, segs), lax.rem(at, segs)
        row = z * lags + lag
        first = pl.multiple_of(s * width, width)
        return lag, tab_ref[0, pl.ds(row, 1), :], tab_ref[1, pl.ds(row, 1), :], first

    def turn(step):
        slab = slab_of(pick(plane_at, step), b)

        def one(at, carry):
            lag, cos_row, sin_row, first = rows_of(at)
            real_part = slabs[slab, :, pl.ds(first, BINS)].astype(jnp.float32)
            imag_part = slabs[slab, :, pl.ds(first + BINS, BINS)].astype(jnp.float32)
            left[step, lag, :, pl.ds(first, BINS)] = (
                cos_row * real_part - sin_row * imag_part
            ).astype(jnp.bfloat16)
            left[step, lag, :, pl.ds(first + BINS, BINS)] = (
                cos_row * imag_part + sin_row * real_part
            ).astype(jnp.bfloat16)
            return carry

        lax.fori_loop(0, lags * segs, one, 0)

    def turn_both(step):
        slab = slab_of(pick(plane_at, step), near_a)

        def one(at, carry):
            lag, cos_row, sin_row, first = rows_of(at)
            group, place = lax.div(lag, 2), part(lax.rem(lag, 2))
            real_part = slabs[slab, part(soon), pl.ds(first, BINS)].astype(jnp.float32)
            imag_part = slabs[slab, part(soon), pl.ds(first + BINS, BINS)].astype(jnp.float32)
            cos_real, sin_imag = cos_row * real_part, sin_row * imag_part
            cos_imag, sin_real = cos_row * imag_part, sin_row * real_part
            for way, (one_part, two_part) in enumerate(
                ((cos_real - sin_imag, cos_imag + sin_real), (cos_real + sin_imag, cos_imag - sin_real))
            ):
                to = left.at[4 + step, way * lags // 2 + group, place]
                to[:, pl.ds(first, BINS)] = one_part.astype(jnp.bfloat16)
                to[:, pl.ds(first + BINS, BINS)] = two_part.astype(jnp.bfloat16)
            return carry

        lax.fori_loop(0, lags * segs, one, 0)

    def pair_of(block):
        return lax.div(block, 2) * 2

    def by_place(end, middle):
        return [
            one if one == two else jnp.where(in_middle, two, one) for one, two in zip(end, middle)
        ]

    codes = by_place(job_codes(END_PHASES), job_codes(MIDDLE_PHASES))
    starts = by_place(job_starts(END_PHASES), job_starts(MIDDLE_PHASES))
    own_turns = by_place(END_TURNS, MIDDLE_TURNS)

    def job(at, carry):
        code = pick(codes, at)
        step, key = lax.div(code, 32), lax.rem(lax.div(code, 8), 4)
        h = pick((0, 1, soon, late), lax.rem(lax.div(code, 2), 4))
        plane = pick(plane_at, step)
        block = pick((b, near_a, near_b, near_b), key)
        arrive(slab_of(plane, block + 1 - 2 * core), h, lax.rem(code, 2) == 1)
        right = slabs[pl.ds(slab_of(plane, pair_of(block)), 2), part(h)]
        term = lax.dot_general(
            left[step + jnp.where(key == 3, 4, 0)].reshape(lags * chans, depth),
            right.reshape(2 * half, depth),
            (((1,), (1,)), ((), ())),
            preferred_element_type=jnp.float32,
        )
        acc[key * 2 + h] += term.reshape(lags, chans, 2 * half)
        return carry

    def finish(at, carry):
        key, h = lax.div(at, 2), lax.rem(at, 2)
        pair = pair_of(pick((b, near_a, near_b), key))
        total = acc[at].astype(jnp.bfloat16)
        for other in range(2):
            first = pl.multiple_of((pair + other) * chans + h * half, half)
            done[:, :, pl.ds(first, half)] = total[:, :, other * half : (other + 1) * half]
        return carry

    def clear(at, carry):
        acc[at] = jnp.zeros(acc.shape[1:], jnp.float32)
        return carry

    pair_b, pair_across = pair_of(near_b), pair_of(across)

    def spot_of(row_half, block, column_half):
        column = pl.multiple_of(block * chans + column_half * half, half)
        return done.at[:, pl.ds(pl.multiple_of(row_half * half, half), half), pl.ds(column, half)]

    def tile_copy(kind, h, t):
        if kind == 0:
            block, spot, at = near_a, spot_of(soon, pair_b + t, h), soon * 4 + h * 2 + t
        else:
            block, spot, at = pair_b + t, spot_of(h, near_a, soon), soon * 4 + h * 2 + core
        return pltpu.make_async_remote_copy(
            src_ref=tiles.at[kind, h, t], dst_ref=spot, send_sem=sent_tile.at[kind * 4 + h * 2 + t],
            recv_sem=got_tile.at[at], device_id=(block, z), device_id_type=MESH,
        )

    def emit(h):
        total = acc[6 + h].reshape(2, lags, half, 2 * half)
        for t in range(2):
            tiles[0, h, t] = total[0, :, :, t * half : (t + 1) * half].astype(jnp.bfloat16)
        for t in range(2):
            tile_copy(0, h, t).start()
        for t in range(2):
            for lag in range(lags):
                tiles[1, h, t, lag] = total[1, lag, :, t * half : (t + 1) * half].T.astype(jnp.bfloat16)
            tile_copy(1, h, t).start()

    mine, slabs_a, slabs_b = [
        [slab_of(plane, block) for plane in plane_at] for block in (b, near_a, near_b)
    ]

    def z_in(step, h, when=None):
        arrive(mine[step], h, when)
        if when is not at_end:
            send(("on", step), mine[step], b, onward[step], h, in_middle)
        send(("z", step, when is at_end), mine[step], sib, z, h, when)

    def xy(step, h, when):
        send(("x", step, when is at_end), mine[step], by_x, z, h, when)
        send(("y", step, when is at_end), mine[step], by_y, z, h, when)

    def take(key, step, h, when=None):
        slab = (slabs_a if key == "A" else slabs_b)[step]
        arrive(slab, h, when)
        if step == 0:
            send((key, "p"), slab, b, partner, h, at_end)
        send((key, step, when is at_end, when is low), slab, sib, z, h, when)

    def land_1():
        z_in(1, 0)
        z_in(2, 0, in_middle)
        xy(1, 0, in_middle)
        take("A", 0, 0)
        take("B", 0, 0)

    def land_2():
        z_in(1, 1)
        z_in(2, 1, in_middle)
        send(("x", 1, True), mine[1], by_x, z, 0, at_end)
        send(("y", 1, True), mine[1], by_y, z, "s", at_end)
        xy(1, 1, in_middle)
        take("A", 0, 1)
        take("B", 0, 1)

    def land_3():
        z_in(2, 0, at_end)
        xy(2, 0, at_end)
        z_in(3, 0, in_middle)
        xy(3, 0, in_middle)
        take("A", 1, "s")
        take("B", 1, 0)

    def land_4():
        z_in(2, 1, at_end)
        xy(2, 1, at_end)
        z_in(3, 1, in_middle)
        xy(3, 1, in_middle)
        send(("B", "m"), slabs_b[0], b, partner, 1, in_middle)
        send(("A", "m"), slabs_a[0], b, partner, "l", in_middle)
        take("A", 2, 0)
        take("B", 2, 0)

    def land_5():
        z_in(3, 0, at_end)
        xy(3, 0, at_end)
        take("A", 2, 1)
        take("B", 2, 1, at_end)

    def land_6():
        z_in(3, 1, at_end)
        xy(3, 1, at_end)
        take("A", 3, 0)
        take("B", 3, 0)
        take("B", 2, 1, in_middle)

    def land_7():
        take("A", 3, 1, high)

    def land_8():
        take("B", 3, 1)
        take("B", 1, 1)
        take("A", 3, 1, low)

    def land_9():
        take("A", 1, "l")

    landings = {1: land_1, 2: land_2, 3: land_3, 4: land_4, 5: land_5, 6: land_6, 7: land_7, 8: land_8, 9: land_9}

    def phase(k, carry):
        for at, land in landings.items():
            pl.when(k == at)(land)
        own_step, near_step = pick(own_turns, k), pick(NEAR_TURNS, k)
        pl.when(own_step > 0)(lambda: turn(own_step - 1))
        pl.when(near_step > 0)(lambda: turn_both(near_step - 1))
        lax.fori_loop(pick(starts, k), pick(starts[1:], k), job, 0)
        pl.when(jnp.logical_and(k >= 7, k <= 8))(lambda: emit(k - 7))
        return carry

    for h in range(2):
        whiten_half(h)
        if h == 0:
            pl.semaphore_wait(barrier, 5 + has_up.astype(jnp.int32) + has_down.astype(jnp.int32))
        send(("up",), own, b, up, h, has_up)
        send(("down",), own, b, down, h, has_down)
        send(("x", 0), own, by_x, z, h)
        send(("y", 0), own, by_y, z, h)
        send(("s", 0), own, sib, z, h)
    lax.fori_loop(0, acc.shape[0], clear, 0)
    lax.fori_loop(0, len(END_TURNS), phase, 0)
    lax.fori_loop(0, 6, finish, 0)

    for side in range(2):
        for h in range(2):
            for t in range(2):
                spot = spot_of(
                    jnp.where(low, h, side), pair_across + t, jnp.where(low, side, h)
                )
                pltpu.make_async_remote_copy(
                    src_ref=tiles.at[0, 0, 0], dst_ref=spot, send_sem=sent_tile.at[0],
                    recv_sem=got_tile.at[side * 4 + h * 2 + t], device_id=(sib, z), device_id_type=MESH,
                ).wait_recv()
    for index, slab, block, plane, h, when in sends.values():
        guarded(when, make(index, slab, block, plane, h).wait_send)
    for kind in range(2):
        for h in range(2):
            for t in range(2):
                tile_copy(kind, h, t).wait_send()


def store(done, out_ref, sem):
    copies = [
        pltpu.make_async_copy(done.at[lag], out_ref.at[lag], sem.at[lag]) for lag in range(done.shape[0])
    ]
    for copy in copies:
        copy.start()
    for copy in copies:
        copy.wait()


def kernel_body(records, glitch_mask, fir_taps):
    blocks, planes = lax.axis_size("blk"), lax.axis_size("tm")
    chans, segs, seglen = records.shape
    seg_total = glitch_mask.shape[1]
    lags_dev = LAGS // planes
    depth = segs * 2 * BINS
    half = chans // 2
    bf16 = jnp.bfloat16
    shape = (lags_dev, chans, chans * blocks)
    done = pl.pallas_call(
        kernel,
        out_shape=pltpu.VMEM(shape, bf16),
        in_specs=[pl.BlockSpec(memory_space=pltpu.VMEM)] * 5,
        out_specs=pl.BlockSpec(memory_space=pltpu.VMEM),
        scratch_shapes=[
            pltpu.VMEM((blocks * planes, chans, depth), bf16),
            pltpu.VMEM((2 * planes, lags_dev, chans, depth), bf16),
            pltpu.VMEM((8, lags_dev, chans, chans), jnp.float32),
            pltpu.VMEM((2, 2, 2, lags_dev, half, half), bf16),
            pltpu.VMEM((8, 128), jnp.float32),
            pltpu.SemaphoreType.DMA((96,)),
            pltpu.SemaphoreType.DMA((blocks * planes, 2)),
            pltpu.SemaphoreType.DMA((8,)),
            pltpu.SemaphoreType.DMA((8,)),
        ],
        compiler_params=pltpu.CompilerParams(
            collective_id=0, has_side_effects=True, vmem_limit_bytes=58 * 1024 * 1024
        ),
        cost_estimate=pl.CostEstimate(
            flops=2 * lags_dev * chans * chans * blocks * planes * depth,
            bytes_accessed=2 * lags_dev * chans * chans * blocks,
            transcendentals=0,
        ),
    )(
        records,
        glitch_mask.T,
        fir_taps[None, :],
        jnp.asarray(dft_thirds(seglen)),
        jnp.asarray(lag_rows(seg_total, seglen)),
    )
    return pl.pallas_call(
        store,
        out_shape=jax.ShapeDtypeStruct(shape, bf16),
        in_specs=[pl.BlockSpec(memory_space=pltpu.VMEM)],
        out_specs=pl.BlockSpec(memory_space=pl.ANY),
        scratch_shapes=[pltpu.SemaphoreType.DMA((lags_dev,))],
        compiler_params=pltpu.CompilerParams(vmem_limit_bytes=4 * 1024 * 1024),
    )(pltpu.with_memory_space_constraint(done, pltpu.VMEM))


def solution(mesh):
    placed = (P("blk", "tm", None), P("blk", None), P())
    small = mesh.shape["blk"] == 8 and mesh.shape["tm"] == 4
    return jax.shard_map(
        kernel_body if small else gathered_body,
        mesh=mesh,
        in_specs=placed,
        out_specs=P("tm", "blk", None),
        check_vma=False,
    )
```

```python
import math

import jax
import jax.numpy as jnp
import numpy as np
from jax import lax
from jax.experimental import pallas as pl
from jax.experimental.pallas import tpu as pltpu
from jax.sharding import PartitionSpec as P

BINS = 128
FIRST_BIN = 16
SMOOTH = 64
LAGS = 16


def dft_thirds(seglen):
    sample = np.arange(seglen)[:, None]
    freq = np.arange(BINS)[None, :] + FIRST_BIN
    angle = (sample * freq % seglen) * (2.0 * math.pi / seglen)
    rest = np.concatenate([np.cos(angle), -np.sin(angle)], axis=1).astype(np.float32)
    thirds = []
    for _ in range(3):
        part = rest.astype(jnp.bfloat16)
        thirds.append(part)
        rest = rest - part.astype(np.float32)
    return np.concatenate(thirds, axis=1)


def lag_rows(seg_total, seglen):
    delay = np.arange(LAGS)[:, None] - LAGS // 2
    freq = np.arange(BINS)[None, :] + FIRST_BIN
    angle = (delay * freq % seglen) * (2.0 * math.pi / seglen)
    factor = 1.0 / math.sqrt(seg_total * BINS)
    tables = np.stack([np.cos(angle), np.sin(angle)]).astype(np.float32) * np.float32(factor)
    return tables.astype(jnp.bfloat16).astype(np.float32)


def filter_matrix(fir_taps, seglen):
    half = (fir_taps.shape[0] - 1) // 2
    period = 2 * seglen
    line = jnp.pad(fir_taps[::-1], (seglen - 1 - half, seglen - half))
    rows = jnp.tile(line, seglen)[: seglen * (period - 1)].reshape(seglen, period - 1)
    return rows[:, seglen - 1 :]


def transform_table(fir_taps, seglen):
    parts = jnp.dot(
        filter_matrix(fir_taps, seglen),
        jnp.asarray(dft_thirds(seglen)),
        preferred_element_type=jnp.float32,
    )
    width = 2 * BINS
    total = parts[:, :width] + (parts[:, width : 2 * width] + parts[:, 2 * width :])
    return total.astype(jnp.bfloat16)


def whiten(samples, usable, fir_taps):
    seglen = samples.shape[1]
    source = lax.broadcasted_iota(jnp.int32, (seglen, seglen), 0)
    target = lax.broadcasted_iota(jnp.int32, (seglen, seglen), 1)
    band_ones = jnp.where(jnp.abs(source - target) <= SMOOTH, 1.0, 0.0).astype(jnp.bfloat16)
    where = lax.broadcasted_iota(jnp.int32, (1, seglen), 1)
    counts = jnp.minimum(where, SMOOTH) + jnp.minimum(seglen - 1 - where, SMOOTH) + 1
    envelope = jnp.dot(
        jnp.abs(samples), band_ones, preferred_element_type=jnp.float32
    ) / counts.astype(jnp.float32)
    normal = (samples.astype(jnp.float32) / (envelope + 1e-06)).astype(jnp.bfloat16)
    spectra = jnp.dot(normal, transform_table(fir_taps, seglen), preferred_element_type=jnp.float32)
    power = jnp.sum(spectra * spectra, axis=1, keepdims=True) * jnp.float32(1.0 / BINS)
    scale = usable.astype(jnp.float32)[:, None] / jnp.sqrt(power + 1e-06)
    return (spectra * scale).astype(jnp.bfloat16)


def gathered_body(records, glitch_mask, fir_taps):
    tm_count = lax.axis_size("tm")
    tm_index = lax.axis_index("tm")
    chans, segs, seglen = records.shape
    seg_total = glitch_mask.shape[1]
    usable = lax.dynamic_slice_in_dim(glitch_mask, tm_index * segs, segs, 1)
    white = whiten(records.reshape(chans * segs, seglen), usable.reshape(chans * segs), fir_taps)
    slab = white.reshape(chans, segs * 2 * BINS)
    column = lax.all_gather(slab, "tm", axis=1, tiled=True)
    every = lax.all_gather(column, "blk", axis=0, tiled=True)
    lags_dev = LAGS // tm_count
    tables = lax.dynamic_slice_in_dim(
        jnp.asarray(lag_rows(seg_total, seglen)), tm_index * lags_dev, lags_dev, 1
    )
    cos_rows = tables[0][:, None, None, :]
    sin_rows = tables[1][:, None, None, :]
    own = column.reshape(chans, seg_total, 2, BINS).astype(jnp.float32)
    real_part, imag_part = own[None, :, :, 0], own[None, :, :, 1]
    turned = jnp.stack(
        [cos_rows * real_part - sin_rows * imag_part, cos_rows * imag_part + sin_rows * real_part],
        axis=3,
    ).astype(jnp.bfloat16)
    left = turned.reshape(lags_dev, chans, seg_total * 2 * BINS)
    return jnp.einsum("lik,jk->lij", left, every, preferred_element_type=jnp.float32).astype(
        jnp.bfloat16
    )


END_PHASES = (
    ("0b01", "0b11",),
    ("0A01", "0B01",),
    ("0A11", "0B11", "0D00", "0D10",),
    ("1b01", "1b11", "1D01",),
    ("1As1", "1B00", "2A01",),
    ("2B01", "2D00", "2D11", "2b01",),
    ("2b11", "2A11", "2B10",),
    ("3D01",),
    ("3A01", "3D11", "1D11",),
    ("3B00", "3A11", "3B10", "1B10", "1Al1", "3b01", "3b11",),
)
MIDDLE_PHASES = (
    ("0b01", "0b11",),
    ("0A01", "0B01",),
    ("0A11", "0B11", "0D00", "0D10",),
    ("1b01", "1b11", "1D01",),
    ("1As1", "1B00", "2A01",),
    ("2B01", "2D00", "2b01", "2b11",),
    ("2D11",),
    ("3D01",),
    ("3A01", "3D11", "1D11",),
    ("2A11", "2B10", "3B00", "3A11", "3B10", "1B10", "1Al1", "3b01", "3b11",),
)
END_TURNS = (1, 0, 0, 2, 3, 0, 4, 0, 0, 0)
MIDDLE_TURNS = (1, 0, 0, 2, 3, 0, 0, 0, 4, 0)
NEAR_TURNS = (0, 0, 1, 2, 0, 3, 0, 4, 0, 0)


def job_codes(phases):
    return [
        int(step) * 32 + "bABD".index(key) * 8 + "01sl".index(h) * 2 + int(waits)
        for line in phases
        for step, key, h, waits in line
    ]


def job_starts(phases):
    return [sum(len(line) for line in phases[:at]) for at in range(len(phases) + 1)]


NEAREST = ((0, 1, 2, 3), (1, 2, 0, 3), (2, 1, 3, 0), (3, 2, 1, 0))
MESH = pl.DeviceIdType.MESH


def kernel(
    x_ref, use_ref, tap_ref, dft_ref, tab_ref, done,
    slabs, left, acc, tiles, taps, sent, got, sent_tile, got_tile,
):
    chans, segs, seglen = x_ref.shape
    width = 2 * BINS
    depth = segs * width
    lags = tab_ref.shape[1] // 4
    half = chans // 2
    part_ch = half // 2
    b, z = lax.axis_index("blk"), lax.axis_index("tm")
    core = lax.rem(b, 2)
    at_x = lax.rem(lax.div(b, 2), 2)
    at_y = lax.div(b, 4)
    sib = b + 1 - 2 * core
    by_x = b + 2 - 4 * at_x
    by_y = b + 4 - 8 * at_y
    across = by_x + 4 - 8 * at_y
    low, high = at_x == 0, at_x == 1
    near_a, near_b = jnp.where(low, by_x, by_y), jnp.where(low, by_y, by_x)
    soon, late = at_x, 1 - at_x
    up, down = z + 1, z - 1
    partner = z + 1 - 2 * lax.rem(z, 2)
    has_up, has_down = z < 3, z > 0
    in_middle = jnp.logical_and(has_up, has_down)
    at_end = jnp.logical_not(in_middle)

    def guarded(when, action):
        if when is None:
            action()
        else:
            pl.when(when)(action)

    barrier = pltpu.get_barrier_semaphore()
    for block, plane, when in (
        (sib, z, None), (by_x, z, None), (by_y, z, None), (b, up, has_up), (b, down, has_down),
        (by_x + 1 - 2 * core, z, None), (by_y + 1 - 2 * core, z, None),
    ):
        guarded(
            when,
            lambda block=block, plane=plane: pl.semaphore_signal(
                barrier, inc=1, device_id=(block, plane), device_id_type=MESH
            ),
        )

    def slab_of(plane, block):
        return plane * 8 + block

    own = slab_of(z, b)
    taps[...] = jnp.zeros_like(taps)
    taps[0:1, : tap_ref.shape[1]] = tap_ref[...].astype(jnp.float32)
    middle = (tap_ref.shape[1] - 1) // 2
    period = 2 * seglen
    tap_at = lax.broadcasted_iota(jnp.int32, (128, period), 0)
    spot = lax.broadcasted_iota(jnp.int32, (128, period), 1)
    offset = middle - tap_at
    place = jnp.where(spot == jnp.where(offset < 0, offset + period, offset), 1.0, 0.0)
    line = jnp.dot(
        taps[...].astype(jnp.bfloat16), place.astype(jnp.bfloat16), preferred_element_type=jnp.float32
    )[0:1]
    line = jnp.broadcast_to(line, (seglen, period))
    fir = pltpu.roll(line, 0, 1, stride=1, stride_axis=0)[:, :seglen].astype(jnp.bfloat16)
    parts = jnp.dot(fir, dft_ref[...], preferred_element_type=jnp.float32)
    table = (parts[:, :width] + (parts[:, width : 2 * width] + parts[:, 2 * width :])).astype(jnp.bfloat16)
    source = lax.broadcasted_iota(jnp.int32, (seglen, seglen), 0)
    target = lax.broadcasted_iota(jnp.int32, (seglen, seglen), 1)
    band_ones = jnp.where(jnp.abs(source - target) <= SMOOTH, 1.0, 0.0).astype(jnp.bfloat16)
    where = lax.broadcasted_iota(jnp.int32, (1, seglen), 1)
    counts = jnp.minimum(where, SMOOTH) + jnp.minimum(seglen - 1 - where, SMOOTH) + 1
    counts = counts.astype(jnp.float32)
    rows = part_ch * segs
    to_row = lax.broadcasted_iota(jnp.int32, (rows, rows), 0)
    from_row = lax.broadcasted_iota(jnp.int32, (rows, rows), 1)
    by_segment = jnp.where(
        from_row == lax.rem(to_row, part_ch) * segs + lax.div(to_row, part_ch), 1.0, 0.0
    ).astype(jnp.bfloat16)
    wanted = lax.broadcasted_iota(jnp.int32, (use_ref.shape[0], segs * BINS), 0)
    column = lax.div(lax.broadcasted_iota(jnp.int32, (use_ref.shape[0], segs * BINS), 1), BINS)
    usable = lax.dot_general(
        use_ref[...].astype(jnp.bfloat16),
        jnp.where(wanted == z * segs + column, 1.0, 0.0).astype(jnp.bfloat16),
        (((0,), (0,)), ((), ())),
        preferred_element_type=jnp.float32,
    )

    def whiten_half(h):
        samples = x_ref[h * half : (h + 1) * half].reshape(half * segs, seglen)
        envelope = jnp.dot(jnp.abs(samples), band_ones, preferred_element_type=jnp.float32) / counts
        normal = (samples.astype(jnp.float32) / (envelope + 1e-06)).astype(jnp.bfloat16)
        spectra = jnp.dot(normal, table, preferred_element_type=jnp.float32)
        power = jnp.sum(spectra * spectra, axis=1, keepdims=True) * jnp.float32(1.0 / BINS)
        white = (spectra / jnp.sqrt(power + 1e-06)).astype(jnp.bfloat16)
        for k in range(2):
            sorted_rows = jnp.dot(
                by_segment, white[k * rows : (k + 1) * rows], preferred_element_type=jnp.float32
            )
            first = h * half + k * part_ch
            for s in range(segs):
                slabs[own, first : first + part_ch, s * width : (s + 1) * width] = (
                    sorted_rows[s * part_ch : (s + 1) * part_ch]
                    * usable[first : first + part_ch, s * BINS : s * BINS + 1]
                ).astype(jnp.bfloat16)

    sends = {}

    def half_of(h):
        return {"s": soon, "l": late}[h] if isinstance(h, str) else h

    def part(h):
        return pl.ds(h * half if isinstance(h, int) else pl.multiple_of(h * half, half), half)

    def make(index, slab, block, plane, h):
        ref = slabs.at[slab, part(half_of(h))]
        return pltpu.make_async_remote_copy(
            src_ref=ref, dst_ref=ref, send_sem=sent.at[index], recv_sem=got.at[slab, half_of(h)],
            device_id=(block, plane), device_id_type=MESH,
        )

    def send(name, slab, block, plane, h, when=None):
        if (name, h) not in sends:
            sends[name, h] = (len(sends), slab, block, plane, h, when)
        guarded(when, lambda: make(*sends[name, h][:-1]).start())

    def arrive(slab, h, when=None):
        guarded(when, lambda: make(0, slab, sib, z, h).wait_recv())

    plane_at, onward = [z], [None]
    for step in range(1, 4):
        plane = sum(jnp.where(z == at, NEAREST[at][step], 0) for at in range(4))
        plane_at.append(plane)
        onward.append(jnp.where(plane > z, z - 1, z + 1))

    def pick(values, index):
        return sum(jnp.where(index == at, value, 0) for at, value in enumerate(values))

    def rows_of(at):
        lag, s = lax.div(at, segs), lax.rem(at, segs)
        row = z * lags + lag
        first = pl.multiple_of(s * width, width)
        return lag, tab_ref[0, pl.ds(row, 1), :], tab_ref[1, pl.ds(row, 1), :], first

    def turn(step):
        slab = slab_of(pick(plane_at, step), b)

        def one(at, carry):
            lag, cos_row, sin_row, first = rows_of(at)
            real_part = slabs[slab, :, pl.ds(first, BINS)].astype(jnp.float32)
            imag_part = slabs[slab, :, pl.ds(first + BINS, BINS)].astype(jnp.float32)
            left[step, lag, :, pl.ds(first, BINS)] = (
                cos_row * real_part - sin_row * imag_part
            ).astype(jnp.bfloat16)
            left[step, lag, :, pl.ds(first + BINS, BINS)] = (
                cos_row * imag_part + sin_row * real_part
            ).astype(jnp.bfloat16)
            return carry

        lax.fori_loop(0, lags * segs, one, 0)

    def turn_both(step):
        slab = slab_of(pick(plane_at, step), near_a)

        def one(at, carry):
            lag, cos_row, sin_row, first = rows_of(at)
            group, place = lax.div(lag, 2), part(lax.rem(lag, 2))
            real_part = slabs[slab, part(soon), pl.ds(first, BINS)].astype(jnp.float32)
            imag_part = slabs[slab, part(soon), pl.ds(first + BINS, BINS)].astype(jnp.float32)
            cos_real, sin_imag = cos_row * real_part, sin_row * imag_part
            cos_imag, sin_real = cos_row * imag_part, sin_row * real_part
            for way, (one_part, two_part) in enumerate(
                ((cos_real - sin_imag, cos_imag + sin_real), (cos_real + sin_imag, cos_imag - sin_real))
            ):
                to = left.at[4 + step, way * lags // 2 + group, place]
                to[:, pl.ds(first, BINS)] = one_part.astype(jnp.bfloat16)
                to[:, pl.ds(first + BINS, BINS)] = two_part.astype(jnp.bfloat16)
            return carry

        lax.fori_loop(0, lags * segs, one, 0)

    def pair_of(block):
        return lax.div(block, 2) * 2

    def by_place(end, middle):
        return [
            one if one == two else jnp.where(in_middle, two, one) for one, two in zip(end, middle)
        ]

    codes = by_place(job_codes(END_PHASES), job_codes(MIDDLE_PHASES))
    starts = by_place(job_starts(END_PHASES), job_starts(MIDDLE_PHASES))
    own_turns = by_place(END_TURNS, MIDDLE_TURNS)

    def job(at, carry):
        code = pick(codes, at)
        step, key = lax.div(code, 32), lax.rem(lax.div(code, 8), 4)
        h = pick((0, 1, soon, late), lax.rem(lax.div(code, 2), 4))
        plane = pick(plane_at, step)
        block = pick((b, near_a, near_b, near_b), key)
        arrive(slab_of(plane, block + 1 - 2 * core), h, lax.rem(code, 2) == 1)
        right = slabs[pl.ds(slab_of(plane, pair_of(block)), 2), part(h)]
        term = lax.dot_general(
            left[step + jnp.where(key == 3, 4, 0)].reshape(lags * chans, depth),
            right.reshape(2 * half, depth),
            (((1,), (1,)), ((), ())),
            preferred_element_type=jnp.float32,
        )
        acc[key * 2 + h] += term.reshape(lags, chans, 2 * half)
        return carry

    def finish(at, carry):
        key, h = lax.div(at, 2), lax.rem(at, 2)
        pair = pair_of(pick((b, near_a, near_b), key))
        total = acc[at].astype(jnp.bfloat16)
        for other in range(2):
            first = pl.multiple_of((pair + other) * chans + h * half, half)
            done[:, :, pl.ds(first, half)] = total[:, :, other * half : (other + 1) * half]
        return carry

    def clear(at, carry):
        acc[at] = jnp.zeros(acc.shape[1:], jnp.float32)
        return carry

    pair_b, pair_across = pair_of(near_b), pair_of(across)

    def spot_of(row_half, block, column_half):
        column = pl.multiple_of(block * chans + column_half * half, half)
        return done.at[:, pl.ds(pl.multiple_of(row_half * half, half), half), pl.ds(column, half)]

    def tile_copy(kind, h, t):
        if kind == 0:
            block, spot, at = near_a, spot_of(soon, pair_b + t, h), soon * 4 + h * 2 + t
        else:
            block, spot, at = pair_b + t, spot_of(h, near_a, soon), soon * 4 + h * 2 + core
        return pltpu.make_async_remote_copy(
            src_ref=tiles.at[kind, h, t], dst_ref=spot, send_sem=sent_tile.at[kind * 4 + h * 2 + t],
            recv_sem=got_tile.at[at], device_id=(block, z), device_id_type=MESH,
        )

    def emit(h):
        total = acc[6 + h].reshape(2, lags, half, 2 * half)
        for t in range(2):
            tiles[0, h, t] = total[0, :, :, t * half : (t + 1) * half].astype(jnp.bfloat16)
        for t in range(2):
            tile_copy(0, h, t).start()
        for t in range(2):
            for lag in range(lags):
                tiles[1, h, t, lag] = total[1, lag, :, t * half : (t + 1) * half].T.astype(jnp.bfloat16)
            tile_copy(1, h, t).start()

    mine, slabs_a, slabs_b = [
        [slab_of(plane, block) for plane in plane_at] for block in (b, near_a, near_b)
    ]

    def z_in(step, h, when=None):
        arrive(mine[step], h, when)
        if when is not at_end:
            send(("on", step), mine[step], b, onward[step], h, in_middle)
        send(("z", step, when is at_end), mine[step], sib, z, h, when)

    def xy(step, h, when):
        send(("x", step, when is at_end), mine[step], by_x, z, h, when)
        send(("y", step, when is at_end), mine[step], by_y, z, h, when)

    def take(key, step, h, when=None):
        slab = (slabs_a if key == "A" else slabs_b)[step]
        arrive(slab, h, when)
        if step == 0:
            send((key, "p"), slab, b, partner, h, at_end)
        send((key, step, when is at_end, when is low), slab, sib, z, h, when)

    def land_1():
        z_in(1, 0)
        z_in(2, 0, in_middle)
        xy(1, 0, in_middle)
        take("A", 0, 0)
        take("B", 0, 0)

    def land_2():
        z_in(1, 1)
        z_in(2, 1, in_middle)
        send(("x", 1, True), mine[1], by_x, z, 0, at_end)
        send(("y", 1, True), mine[1], by_y, z, "s", at_end)
        xy(1, 1, in_middle)
        take("A", 0, 1)
        take("B", 0, 1)

    def land_3():
        z_in(2, 0, at_end)
        xy(2, 0, at_end)
        z_in(3, 0, in_middle)
        xy(3, 0, in_middle)
        take("A", 1, "s")
        take("B", 1, 0)

    def land_4():
        z_in(2, 1, at_end)
        xy(2, 1, at_end)
        z_in(3, 1, in_middle)
        xy(3, 1, in_middle)
        send(("B", "m"), slabs_b[0], b, partner, 1, in_middle)
        send(("A", "m"), slabs_a[0], b, partner, "l", in_middle)
        take("A", 2, 0)
        take("B", 2, 0)

    def land_5():
        z_in(3, 0, at_end)
        xy(3, 0, at_end)
        take("A", 2, 1)
        take("B", 2, 1, at_end)

    def land_6():
        z_in(3, 1, at_end)
        xy(3, 1, at_end)
        take("A", 3, 0)
        take("B", 3, 0)
        take("B", 2, 1, in_middle)

    def land_7():
        take("A", 3, 1, high)

    def land_8():
        take("B", 3, 1)
        take("B", 1, 1)
        take("A", 3, 1, low)

    def land_9():
        take("A", 1, "l")

    landings = {1: land_1, 2: land_2, 3: land_3, 4: land_4, 5: land_5, 6: land_6, 7: land_7, 8: land_8, 9: land_9}

    def phase(k, carry):
        for at, land in landings.items():
            pl.when(k == at)(land)
        own_step, near_step = pick(own_turns, k), pick(NEAR_TURNS, k)
        pl.when(own_step > 0)(lambda: turn(own_step - 1))
        pl.when(near_step > 0)(lambda: turn_both(near_step - 1))
        lax.fori_loop(pick(starts, k), pick(starts[1:], k), job, 0)
        pl.when(jnp.logical_and(k >= 7, k <= 8))(lambda: emit(k - 7))
        return carry

    for h in range(2):
        whiten_half(h)
        if h == 0:
            pl.semaphore_wait(barrier, 5 + has_up.astype(jnp.int32) + has_down.astype(jnp.int32))
        send(("up",), own, b, up, h, has_up)
        send(("down",), own, b, down, h, has_down)
        send(("x", 0), own, by_x, z, h)
        send(("y", 0), own, by_y, z, h)
        send(("s", 0), own, sib, z, h)
    lax.fori_loop(0, acc.shape[0], clear, 0)
    lax.fori_loop(0, len(END_TURNS), phase, 0)
    lax.fori_loop(0, 6, finish, 0)

    for index, slab, block, plane, h, when in sends.values():
        guarded(when, make(index, slab, block, plane, h).wait_send)
    for side in range(2):
        for h in range(2):
            for t in range(2):
                spot = spot_of(
                    jnp.where(low, h, side), pair_across + t, jnp.where(low, side, h)
                )
                pltpu.make_async_remote_copy(
                    src_ref=tiles.at[0, 0, 0], dst_ref=spot, send_sem=sent_tile.at[0],
                    recv_sem=got_tile.at[side * 4 + h * 2 + t], device_id=(sib, z), device_id_type=MESH,
                ).wait_recv()
    for kind in range(2):
        for h in range(2):
            for t in range(2):
                tile_copy(kind, h, t).wait_send()


def store(done, out_ref, sem):
    copies = [
        pltpu.make_async_copy(done.at[lag], out_ref.at[lag], sem.at[lag]) for lag in range(done.shape[0])
    ]
    for copy in copies:
        copy.start()
    for copy in copies:
        copy.wait()


def kernel_body(records, glitch_mask, fir_taps):
    blocks, planes = lax.axis_size("blk"), lax.axis_size("tm")
    chans, segs, seglen = records.shape
    seg_total = glitch_mask.shape[1]
    lags_dev = LAGS // planes
    depth = segs * 2 * BINS
    half = chans // 2
    bf16 = jnp.bfloat16
    shape = (lags_dev, chans, chans * blocks)
    done = pl.pallas_call(
        kernel,
        out_shape=pltpu.VMEM(shape, bf16),
        in_specs=[pl.BlockSpec(memory_space=pltpu.VMEM)] * 5,
        out_specs=pl.BlockSpec(memory_space=pltpu.VMEM),
        scratch_shapes=[
            pltpu.VMEM((blocks * planes, chans, depth), bf16),
            pltpu.VMEM((2 * planes, lags_dev, chans, depth), bf16),
            pltpu.VMEM((8, lags_dev, chans, chans), jnp.float32),
            pltpu.VMEM((2, 2, 2, lags_dev, half, half), bf16),
            pltpu.VMEM((8, 128), jnp.float32),
            pltpu.SemaphoreType.DMA((96,)),
            pltpu.SemaphoreType.DMA((blocks * planes, 2)),
            pltpu.SemaphoreType.DMA((8,)),
            pltpu.SemaphoreType.DMA((8,)),
        ],
        compiler_params=pltpu.CompilerParams(
            collective_id=0, has_side_effects=True, vmem_limit_bytes=58 * 1024 * 1024
        ),
        cost_estimate=pl.CostEstimate(
            flops=2 * lags_dev * chans * chans * blocks * planes * depth,
            bytes_accessed=2 * lags_dev * chans * chans * blocks,
            transcendentals=0,
        ),
    )(
        records,
        glitch_mask.T,
        fir_taps[None, :],
        jnp.asarray(dft_thirds(seglen)),
        jnp.asarray(lag_rows(seg_total, seglen)),
    )
    return pl.pallas_call(
        store,
        out_shape=jax.ShapeDtypeStruct(shape, bf16),
        in_specs=[pl.BlockSpec(memory_space=pltpu.VMEM)],
        out_specs=pl.BlockSpec(memory_space=pl.ANY),
        scratch_shapes=[pltpu.SemaphoreType.DMA((lags_dev,))],
        compiler_params=pltpu.CompilerParams(vmem_limit_bytes=4 * 1024 * 1024),
    )(pltpu.with_memory_space_constraint(done, pltpu.VMEM))


def solution(mesh):
    placed = (P("blk", "tm", None), P("blk", None), P())
    small = mesh.shape["blk"] == 8 and mesh.shape["tm"] == 4
    return jax.shard_map(
        kernel_body if small else gathered_body,
        mesh=mesh,
        in_specs=placed,
        out_specs=P("tm", "blk", None),
        check_vma=False,
    )
```
